512 devices in a mesh: context: 32 (over z_hi, y, core), tensor: 16 (over z_lo, x).
Axes of the slice: x: 4, y: 8, z: 8 (z_hi: 2, z_lo: 4; z = z_hi * 4 + z_lo), core: 2. Of those that a mesh axis runs over, the one named last changes fastest.
Arguments:
- queries: bfloat16 [8192, 16384], P('context', 'tensor')
- key_value_rows: bfloat16 [2, 8192, 1024], P(None, ('context', 'tensor'))
- positions: int32 [8192], P('context'), may hold values from 0 to 8191, as said below
Outputs:
- attended: bfloat16 [8192, 16384], P(('context', 'tensor'))
The draws below stay inside these ranges and needn't reach their ends.
Inputs may be any that keep to these rules, and one draw needn't show every extreme that they name: positions is a permutation of 0 .. 8191 made of 64 blocks of 128 consecutive rising positions; each aligned run of 256 tokens holds block j and block 63 - j for some j, in either order.
All inputs are finite; a program needn't handle non-finite values.
Results may differ from the reference program's by a relative error of at most 0.007.
Values may be sent and summed in bfloat16 or wider, within the bound.
A program may use at most 64 MiB of HBM per device.

```python
import math
import jax
import jax.numpy as jnp
from jax import lax

HEAD_SIZE = 128
TOK_DEV = 256
QUERY_HEADS = 128
KEY_VALUE_HEADS = 8
SLAB_TOKENS = 8192


def shared_keys(key):
    return jnp.clip(jax.random.normal(key, (SLAB_TOKENS, KEY_VALUE_HEADS * HEAD_SIZE), jnp.float32), -6.0, 6.0)


def draw_key_value_rows(key, part):
    rotary_base = shared_keys(key)
    key = jax.random.fold_in(key, 11)
    value_matrix = jnp.clip(jax.random.normal(key, (SLAB_TOKENS, KEY_VALUE_HEADS * HEAD_SIZE), jnp.float32), -6.0, 6.0)
    return jnp.stack([rotary_base, value_matrix]).astype(jnp.bfloat16)


def draw_queries(key, part):
    key = jax.random.fold_in(key, 5)
    drawn = jnp.clip(jax.random.normal(key, (SLAB_TOKENS, QUERY_HEADS * HEAD_SIZE), jnp.float32), -6.0, 6.0)
    return drawn.astype(jnp.bfloat16)


def draw_positions(key, part):
    key = jax.random.fold_in(key, 3)
    slices = SLAB_TOKENS // TOK_DEV
    half_rows = TOK_DEV // 2
    order = jax.random.permutation(key, slices)
    flipped = jax.random.randint(jax.random.fold_in(key, 1), (slices,), 0, 2)
    first = jnp.where(flipped == 0, order, 2 * slices - 1 - order)
    second = 2 * slices - 1 - first
    block_ids = jnp.stack([first, second], axis=1).reshape(-1)
    places = block_ids[:, None] * half_rows + jnp.arange(half_rows)[None, :]
    return places.reshape(-1).astype(jnp.int32)


def setup_inputs(seed: int = 0) -> dict:
    key_list = jax.random.split(jax.random.key(seed), 4)
    return {
        "queries": draw_queries(jax.random.fold_in(key_list[3], 71), 0),
        "key_value_rows": draw_key_value_rows(jax.random.fold_in(key_list[3], 71), 0),
        "positions": draw_positions(jax.random.fold_in(key_list[3], 71), 0),
    }


NEGATIVE = -1e+30

def frequencies(width):
    counter = jnp.arange(width // 2, dtype=jnp.float32)
    inverse = 500000.0 ** (-2.0 * counter / width)
    wavelength = 2.0 * math.pi / inverse
    smooth = jnp.clip((8192.0 / wavelength - 1.0) / 3.0, 0.0, 1.0)
    return (1.0 - smooth) * inverse / 8.0 + smooth * inverse

def apply_rotary(value_matrix, places):
    width = value_matrix.shape[-1]
    half_width = width // 2
    angles = places.astype(jnp.float32)[:, None] * frequencies(width)[None, :]
    angles = angles.reshape((value_matrix.shape[0],) + (1,) * (value_matrix.ndim - 2) + (half_width,))
    cosine = jnp.cos(angles)
    sine = jnp.sin(angles)
    first = value_matrix[..., :half_width].astype(jnp.float32)
    second = value_matrix[..., half_width:].astype(jnp.float32)
    return jnp.concatenate([first * cosine - second * sine, second * cosine + first * sine], axis=-1)

def reference(queries, key_value_rows, positions):
    rotated_q = apply_rotary(queries.reshape(SLAB_TOKENS, QUERY_HEADS, HEAD_SIZE), positions).astype(jnp.bfloat16)
    turned_keys = apply_rotary(key_value_rows[0].reshape(SLAB_TOKENS, KEY_VALUE_HEADS, HEAD_SIZE), positions).astype(jnp.bfloat16)
    value_head_rows = key_value_rows[1].reshape(SLAB_TOKENS, KEY_VALUE_HEADS, HEAD_SIZE)
    query_group = QUERY_HEADS // KEY_VALUE_HEADS
    block_rows = min(SLAB_TOKENS, 1024)
    blocks = SLAB_TOKENS // block_rows
    scale = 1.0 / math.sqrt(HEAD_SIZE)

    def per_head(head):
        query_all = lax.dynamic_index_in_dim(rotated_q, head, 1, keepdims=False)
        key_all = lax.dynamic_index_in_dim(turned_keys, head // query_group, 1, keepdims=False)
        value_all = lax.dynamic_index_in_dim(value_head_rows, head // query_group, 1, keepdims=False)

        def per_block(number):
            first_row = (number * block_rows).astype(jnp.int32)
            query_rows = lax.dynamic_slice_in_dim(query_all, first_row, block_rows, 0)
            query_places = lax.dynamic_slice_in_dim(positions, first_row, block_rows, 0)
            scores = jnp.dot(query_rows, key_all.T, preferred_element_type=jnp.float32) * scale
            visible = positions[None, :] <= query_places[:, None]
            scores = jnp.where(visible, scores, NEGATIVE)
            highest = lax.optimization_barrier(jnp.max(scores, axis=1, keepdims=True))
            weights = jnp.where(visible, jnp.exp(scores - highest), 0.0)
            totals = lax.optimization_barrier(jnp.sum(weights, axis=1, keepdims=True))
            mixed = jnp.dot(weights.astype(jnp.bfloat16), value_all, preferred_element_type=jnp.float32) / totals
            return mixed.astype(jnp.bfloat16)
        return lax.map(per_block, jnp.arange(blocks, dtype=jnp.int32)).reshape(SLAB_TOKENS, HEAD_SIZE)
    heads_out = lax.map(per_head, jnp.arange(QUERY_HEADS, dtype=jnp.int32))
    return jnp.transpose(heads_out, (1, 0, 2)).reshape(SLAB_TOKENS, QUERY_HEADS * HEAD_SIZE)
```

```python
import functools
import math

import jax
import jax.numpy as jnp
import numpy as np
from jax import lax
from jax.experimental import pallas as pl
from jax.experimental.pallas import tpu as pltpu
from jax.sharding import PartitionSpec as P

HEAD = 128
BLOCK = 128
SLICE = 2 * BLOCK
NEGATIVE = -1e30
POSITIVE = 1e30
MESH = pl.DeviceIdType.MESH
F32 = jnp.float32
BF16 = jnp.bfloat16


LAYERS = ((0, 2 * BLOCK), (2 * BLOCK, 2 * BLOCK + 16))
SLOT = 4 * BLOCK + 16


def frequencies(width):
    counter = np.arange(width // 2, dtype=np.float32)
    inverse = np.float32(500000.0) ** (np.float32(-2.0) * counter / np.float32(width))
    wavelength = np.float32(2.0 * math.pi) / inverse
    smooth = np.clip((np.float32(8192.0) / wavelength - 1) / 3, 0, 1)
    f = (1 - smooth) * inverse / 8 + smooth * inverse
    return np.broadcast_to(np.concatenate([f, f])[None, :], (8, width)).astype(np.float32)


def dot_nn(a, b):
    return jnp.dot(a, b, preferred_element_type=F32)


def kernel(
    contexts, ranks, heads, block_rows,
    q_ref, kv_ref, place_ref, freq_ref, out_ref,
    queries, landed, slab, staged, qq, keys_one, keys_two, vals_big, vals_small, bias,
    out_big, out_small, max_big, max_small, done,
    q_sem, a_send, a_recv, m_send, m_recv, r_send, r_recv, s_send, s_recv, o_send, o_recv,
):
    ring = contexts // 4
    group = SLICE // ranks
    half_groups = ranks // 2
    plane = 2 * ranks
    blocks = 2 * contexts
    scale = math.log2(math.e) / math.sqrt(HEAD)

    c = lax.axis_index("context")
    t = lax.axis_index("tensor")
    core = lax.rem(c, 2)
    y = lax.rem(lax.div(c, 2), ring)
    z = lax.div(c, 2 * ring)
    way = 1 - 2 * core

    def at(zz, yy, cc):
        return (zz * ring + yy) * 2 + cc

    def turn(v):
        return lax.rem(v + 2 * ring, ring)

    following = at(z, turn(y + way), core)
    previous = at(z, turn(y - way), core)
    sibling = at(z, y, 1 - core)
    across = at(1 - z, y, core)
    me = z * ranks + t

    def near(k):
        pt = lax.rem(t + k, ranks)
        return z * ranks + pt, c, pt

    def far(k):
        pt = lax.rem(t + k, ranks)
        return (1 - z) * ranks + pt, across, pt

    barrier = pltpu.get_barrier_semaphore()

    def greet_near(k, carry):
        p, pc, pt = near(k)
        pl.semaphore_signal(barrier, inc=1, device_id=(pc, pt), device_id_type=MESH)
        return carry

    def greet_far(k, carry):
        p, pc, pt = far(k)
        pl.semaphore_signal(barrier, inc=1, device_id=(pc, pt), device_id_type=MESH)
        return carry

    lax.fori_loop(1, ranks, greet_near, 0)
    lax.fori_loop(0, ranks, greet_far, 0)
    for neighbour in (following, previous, sibling):
        pl.semaphore_signal(barrier, inc=1, device_id=(neighbour, t), device_id_type=MESH)

    fetch = pltpu.make_async_copy(q_ref, queries, q_sem.at[0])
    fetch.start()

    def number(half):
        return jnp.right_shift(place_ref[pl.ds(half, 1), :], 7).astype(F32)

    def rotation(block_number, start, rows):
        step = lax.broadcasted_iota(jnp.int32, (rows, HEAD), 0) + start
        angle = (block_number * BLOCK + step.astype(F32)) * freq_ref[0:1, :]
        lane = lax.broadcasted_iota(jnp.int32, (rows, HEAD), 1)
        return jnp.cos(angle), jnp.where(lane < HEAD // 2, -1.0, 1.0) * jnp.sin(angle)

    cos_k, sin_k = rotation(
        number(lax.div(t, half_groups)), lax.rem(t, half_groups) * group, group
    )
    for h in range(ranks // 2):
        cols = slice(h * HEAD, (h + 1) * HEAD)
        x = kv_ref[0, :, cols].astype(F32)
        staged[h, 0] = (x * cos_k + pltpu.roll(x, HEAD // 2, 1) * sin_k).astype(BF16)
        staged[h, 1] = kv_ref[1, :, cols]
    landed[z, 2 * ranks] = jnp.broadcast_to(number(0), (group, HEAD)).astype(BF16)
    mine_now = staged[lax.div(t, 2)]
    landed[z, 2 * t] = mine_now[0]
    landed[z, 2 * t + 1] = mine_now[1]

    pl.semaphore_wait(barrier, plane - 1 + 3)

    def plane_copy(peer):
        p, pc, pt = peer
        return pltpu.make_async_remote_copy(
            src_ref=staged.at[lax.div(pt, 2)],
            dst_ref=landed.at[z, pl.ds(2 * t, 2)],
            send_sem=a_send.at[p],
            recv_sem=a_recv.at[me],
            device_id=(pc, pt),
            device_id_type=MESH,
        )

    def near_start(k, carry):
        plane_copy(near(k)).start()
        return carry

    def far_start(k, carry):
        plane_copy(far(k)).start()
        return carry

    def id_copy(zz):
        return pltpu.make_async_remote_copy(
            src_ref=landed.at[zz, 2 * ranks],
            dst_ref=landed.at[zz, 2 * ranks],
            send_sem=m_send.at[0],
            recv_sem=m_recv.at[0],
            device_id=(across, t),
            device_id_type=MESH,
        )

    lax.fori_loop(1, ranks, near_start, 0)
    id_copy(z).start()
    lax.fori_loop(0, ranks, far_start, 0)

    def plane_wait(zz, pt):
        pltpu.make_async_remote_copy(
            src_ref=staged.at[0],
            dst_ref=landed.at[zz, pl.ds(2 * pt, 2)],
            send_sem=a_send.at[0],
            recv_sem=a_recv.at[zz * ranks + pt],
            device_id=(across, t),
            device_id_type=MESH,
        ).wait_recv()

    def near_wait(k, carry):
        plane_wait(z, lax.rem(t + k, ranks))
        return carry

    def far_wait(k, carry):
        plane_wait(1 - z, lax.rem(t + k, ranks))
        return carry

    def slot(r, s):
        return at(lax.rem(z + s, 2), turn(y - way * r), core)

    def slot_sibling(r, s):
        return at(lax.rem(z + s, 2), turn(y + way * r), 1 - core)

    def move(where, layer, send, recv, target):
        low, high = LAYERS[layer]
        view = slab.at[where, pl.ds(low, high)]
        return pltpu.make_async_remote_copy(
            src_ref=view, dst_ref=view, send_sem=send, recv_sem=recv,
            device_id=(target, t), device_id_type=MESH,
        )

    def ring_copy(r, s, layer):
        e = 2 * s + layer
        return move(slot(r, s), layer, r_send.at[r, e], r_recv.at[r + 1, e], following)

    def ring_wait(r, s, layer):
        e = 2 * s + layer
        move(slot(r, s), layer, r_send.at[r, e], r_recv.at[r, e], following).wait_recv()

    def sibling_copy(r, s, layer):
        e = 2 * s + layer
        return move(slot(r, s), layer, s_send.at[r, e], s_recv.at[r, e], sibling)

    def sibling_wait(r, s, layer):
        e = 2 * s + layer
        where = slot_sibling(r, s)
        move(where, layer, s_send.at[r, e], s_recv.at[r, e], sibling).wait_recv()

    def arrange(zz):
        where = at(zz, y, core)
        first = landed[zz, 2 * ranks].astype(F32)[0:1, :]
        smaller = first < blocks / 2
        halves = []
        for plane_index in range(2):
            pair = []
            for i in range(2):
                pieces = [
                    landed[zz, 2 * (i * half_groups + g) + plane_index] for g in range(half_groups)
                ]
                pair.append(jnp.concatenate(pieces, axis=0).astype(F32))
            halves.append(jnp.where(smaller, pair[0], pair[1]))
            halves.append(jnp.where(smaller, pair[1], pair[0]))
        slab[where, 0:BLOCK] = halves[0].T.astype(BF16)
        slab[where, BLOCK:2 * BLOCK] = halves[1].T.astype(BF16)
        slab[where, 2 * BLOCK:3 * BLOCK] = halves[2].astype(BF16)
        slab[where, 3 * BLOCK:4 * BLOCK] = halves[3].astype(BF16)
        low = jnp.minimum(first, blocks - 1 - first)
        slab[where, 4 * BLOCK:SLOT] = jnp.broadcast_to(low, (16, HEAD)).astype(BF16)

    def launch(s):
        for layer in range(2):
            ring_copy(0, s, layer).start()
            sibling_copy(0, s, layer).start()

    lax.fori_loop(1, ranks, near_wait, 0)
    arrange(z)
    launch(0)

    first_id = number(0)
    first_small = first_id < blocks / 2
    my_small = jnp.minimum(first_id, blocks - 1 - first_id)
    fetch.wait()
    turns = [rotation(number(i), 0, BLOCK) for i in range(2)]
    for h in range(heads):
        rows = slice(h * BLOCK, (h + 1) * BLOCK)
        turned = []
        for i in range(2):
            x = queries[i * BLOCK:(i + 1) * BLOCK, h * HEAD:(h + 1) * HEAD].astype(F32)
            turned.append(x * turns[i][0] + pltpu.roll(x, HEAD // 2, 1) * turns[i][1])
        qq[rows, 0:HEAD] = jnp.where(first_small, turned[0], turned[1]).astype(BF16)
        qq[rows, HEAD:2 * HEAD] = jnp.where(first_small, turned[1], turned[0]).astype(BF16)

    lax.fori_loop(0, ranks, far_wait, 0)
    id_copy(1 - z).wait_recv()
    arrange(1 - z)
    launch(1)

    ones = jnp.ones((BLOCK, HEAD), BF16)
    token = lax.broadcasted_iota(jnp.int32, (BLOCK, BLOCK), 0)
    key = lax.broadcasted_iota(jnp.int32, (BLOCK, BLOCK), 1)

    def diagonal(h, carry):
        rows = pl.ds(pl.multiple_of(h * BLOCK, BLOCK), BLOCK)
        for i, (best, total) in enumerate(((max_small, out_small), (max_big, out_big))):
            s = dot_nn(qq[rows, i * HEAD:(i + 1) * HEAD], slab[c, i * BLOCK:(i + 1) * BLOCK])
            s = jnp.where(key <= token, s, NEGATIVE)
            m = jnp.max(s, axis=1, keepdims=True)
            best[rows, :] = jnp.broadcast_to(m, (BLOCK, HEAD))
            values = jnp.concatenate(
                [slab[c, (2 + i) * BLOCK:(3 + i) * BLOCK], ones], axis=1
            )
            total[rows, :] = dot_nn(jnp.exp2((s - m) * scale).astype(BF16), values)
        return carry

    lax.fori_loop(0, heads, diagonal, 0)
    for i in range(4):
        vals_big[i * BLOCK:(i + 1) * BLOCK, HEAD:2 * HEAD] = ones

    def flag(condition):
        return jnp.where(condition, 1.0, 0.0)

    def prepare(r):
        places = (slot(r, 0), slot(r, 1), slot_sibling(r, 0), slot_sibling(r, 1))
        for i, where in enumerate(places):
            small = slab[where, 4 * BLOCK:SLOT].astype(F32)[0:1, :]
            low = flag(small < my_small)
            high = flag(small > my_small)
            bias[2 * i] = jnp.broadcast_to((high - 1.0) * POSITIVE, (8, HEAD))
            bias[2 * i + 1] = jnp.broadcast_to((low - 1.0) * POSITIVE, (8, HEAD))
            low = low.astype(BF16)
            high = high.astype(BF16)
            span = slice(i * BLOCK, (i + 1) * BLOCK)
            later = slice((4 + i) * BLOCK, (5 + i) * BLOCK)
            k_small = slab[where, 0:BLOCK]
            k_big = slab[where, BLOCK:2 * BLOCK]
            v_small = slab[where, 2 * BLOCK:3 * BLOCK]
            v_big = slab[where, 3 * BLOCK:4 * BLOCK]
            keys_one[:, span] = k_small
            keys_two[0:HEAD, span] = k_small * low
            keys_two[HEAD:2 * HEAD, span] = k_big * high
            vals_big[span, 0:HEAD] = v_small
            vals_big[later, 0:HEAD] = v_big * high
            vals_big[later, HEAD:2 * HEAD] = ones * high
            vals_small[span, 0:HEAD] = v_small * low
            vals_small[span, HEAD:2 * HEAD] = ones * low

    def advance(starts):
        bias_big = [bias[2 * i][0:1, :] for i in range(4)]
        bias_small = [bias[2 * i + 1][0:1, :] for i in range(4)]
        scores = []
        for start in starts:
            q = qq[start:start + block_rows, :]
            scores.append((dot_nn(q[:, HEAD:2 * HEAD], keys_one[...]), dot_nn(q, keys_two[...])))
        for start, (one, two) in zip(starts, scores):
            rows = slice(start, start + block_rows)
            ones_of = [one[:, i * BLOCK:(i + 1) * BLOCK] for i in range(4)]
            twos_of = [two[:, i * BLOCK:(i + 1) * BLOCK] for i in range(4)]
            big = functools.reduce(
                jnp.maximum, ones_of + [x + w for x, w in zip(twos_of, bias_big)]
            )
            small = functools.reduce(
                jnp.maximum, [x + w for x, w in zip(twos_of, bias_small)]
            )
            old_big = max_big[rows, :]
            old_small = max_small[rows, :]
            new_big = jnp.maximum(old_big, jnp.max(big, axis=1, keepdims=True))
            new_small = jnp.maximum(old_small, jnp.max(small, axis=1, keepdims=True))
            max_big[rows, :] = new_big
            max_small[rows, :] = new_small
            alpha_big = jnp.exp2((old_big - new_big) * scale)
            alpha_small = jnp.exp2((old_small - new_small) * scale)
            weights = [jnp.exp2((x - new_big) * scale).astype(BF16) for x in ones_of]
            later = []
            for x, wb, ws in zip(twos_of, bias_big, bias_small):
                m = jnp.where(wb == 0.0, new_big, jnp.where(ws == 0.0, new_small, POSITIVE))
                later.append(jnp.exp2((x - m) * scale).astype(BF16))
            later = jnp.concatenate(later, axis=1)
            every = jnp.concatenate(weights + [later], axis=1)
            wide_big = jnp.concatenate([alpha_big, alpha_big], axis=1)
            wide_small = jnp.concatenate([alpha_small, alpha_small], axis=1)
            out_big[rows, :] = out_big[rows, :] * wide_big + dot_nn(every, vals_big[...])
            out_small[rows, :] = out_small[rows, :] * wide_small + dot_nn(later, vals_small[...])

    half_heads = heads // 2
    width = half_heads * HEAD

    def columns(rank, s):
        return pl.ds(pl.multiple_of((2 * rank + s) * width, width), width)

    def tokens(rank):
        return pl.ds(pl.multiple_of(rank * group, group), group)

    def out_move(src, dst, s, send, recv, target):
        return pltpu.make_async_remote_copy(
            src_ref=done.at[tokens(src), pl.ds(s * width, width)],
            dst_ref=out_ref.at[:, columns(dst, s)],
            send_sem=o_send.at[send, s],
            recv_sem=o_recv.at[recv, s],
            device_id=(c, target),
            device_id_type=MESH,
        )

    def finish(s):
        for h in range(s * half_heads, (s + 1) * half_heads):
            rows = slice(h * BLOCK, (h + 1) * BLOCK)
            cols = slice(h * HEAD, (h + 1) * HEAD)
            small = out_small[rows, 0:HEAD] / out_small[rows, HEAD:2 * HEAD]
            big = out_big[rows, 0:HEAD] / out_big[rows, HEAD:2 * HEAD]
            done[0:BLOCK, cols] = jnp.where(first_small, small, big).astype(BF16)
            done[BLOCK:SLICE, cols] = jnp.where(first_small, big, small).astype(BF16)

        def out_start(k, carry):
            pt = lax.rem(t + k, ranks)
            out_move(pt, t, s, pt, t, pt).start()
            return carry

        lax.fori_loop(1, ranks, out_start, 0)
        out_ref[:, columns(t, s)] = done[tokens(t), s * width:(s + 1) * width]

    half_rows = heads * BLOCK // 2

    def step(r, carry):
        for s in range(2):
            for layer in range(2):
                sibling_wait(r, s, layer)
        prepare(r)
        for s in range(2):

            @pl.when(r < ring - 1)
            def _():
                for layer in range(2):
                    ring_wait(r + 1, s, layer)

                    @pl.when(r < ring - 2)
                    def _():
                        ring_copy(r + 1, s, layer).start()

                    sibling_copy(r + 1, s, layer).start()

            advance(range(s * half_rows, (s + 1) * half_rows, block_rows))

            @pl.when(r == ring - 1)
            def _():
                finish(s)

        return carry

    lax.fori_loop(0, ring, step, 0)

    def near_sent(k, carry):
        plane_copy(near(k)).wait_send()
        return carry

    def far_sent(k, carry):
        plane_copy(far(k)).wait_send()
        return carry

    def ring_sent(r, carry):
        for s in range(2):
            for layer in range(2):
                ring_copy(r, s, layer).wait_send()
        return carry

    def sibling_sent(r, carry):
        for s in range(2):
            for layer in range(2):
                sibling_copy(r, s, layer).wait_send()
        return carry

    def out_sent(k, carry):
        pt = lax.rem(t + k, ranks)
        for s in range(2):
            out_move(pt, t, s, pt, t, pt).wait_send()
        return carry

    def out_wait(k, carry):
        pt = lax.rem(t + k, ranks)
        for s in range(2):
            out_move(t, pt, s, t, pt, pt).wait_recv()
        return carry

    lax.fori_loop(1, ranks, near_sent, 0)
    lax.fori_loop(0, ranks, far_sent, 0)
    id_copy(z).wait_send()
    lax.fori_loop(0, ring - 1, ring_sent, 0)
    lax.fori_loop(0, ring, sibling_sent, 0)
    lax.fori_loop(1, ranks, out_sent, 0)
    lax.fori_loop(1, ranks, out_wait, 0)


def local(contexts, ranks, queries, key_value_rows, positions):
    heads = queries.shape[1] // HEAD
    group = SLICE // ranks
    ring = contexts // 4
    rows = heads * BLOCK
    block_rows = min(256, rows // 4)
    dma = pltpu.SemaphoreType.DMA
    vmem = pl.BlockSpec(memory_space=pltpu.VMEM)
    return pl.pallas_call(
        functools.partial(kernel, contexts, ranks, heads, block_rows),
        out_shape=jax.ShapeDtypeStruct((group, ranks * heads * HEAD), BF16),
        in_specs=[pl.BlockSpec(memory_space=pl.ANY), vmem, vmem, vmem],
        out_specs=vmem,
        scratch_shapes=[
            pltpu.VMEM((SLICE, heads * HEAD), BF16),
            pltpu.VMEM((2, 2 * ranks + 1, group, HEAD), BF16),
            pltpu.VMEM((contexts, SLOT, HEAD), BF16),
            pltpu.VMEM((ranks // 2, 2, group, HEAD), BF16),
            pltpu.VMEM((rows, 2 * HEAD), BF16),
            pltpu.VMEM((HEAD, 4 * BLOCK), BF16),
            pltpu.VMEM((2 * HEAD, 4 * BLOCK), BF16),
            pltpu.VMEM((8 * BLOCK, 2 * HEAD), BF16),
            pltpu.VMEM((4 * BLOCK, 2 * HEAD), BF16),
            pltpu.VMEM((8, 8, HEAD), F32),
            pltpu.VMEM((rows, 2 * HEAD), F32),
            pltpu.VMEM((rows, 2 * HEAD), F32),
            pltpu.VMEM((rows, HEAD), F32),
            pltpu.VMEM((rows, HEAD), F32),
            pltpu.VMEM((SLICE, heads * HEAD), BF16),
            dma((1,)),
            dma((2 * ranks,)),
            dma((2 * ranks,)),
            dma((1,)),
            dma((1,)),
            dma((ring, 4)),
            dma((ring, 4)),
            dma((ring, 4)),
            dma((ring, 4)),
            dma((ranks, 2)),
            dma((ranks, 2)),
        ],
        compiler_params=pltpu.CompilerParams(
            collective_id=0, has_side_effects=True, vmem_limit_bytes=48 * 1024 * 1024
        ),
        cost_estimate=pl.CostEstimate(
            flops=8 * rows * SLICE * contexts * HEAD // 2,
            bytes_accessed=4 * 1024 * 1024,
            transcendentals=rows * SLICE * contexts,
        ),
    )(queries, key_value_rows, positions.reshape(2, BLOCK), jnp.asarray(frequencies(HEAD)))


def solution(mesh):
    placed = (P("context", "tensor"), P(None, ("context", "tensor"), None), P("context"))
    return jax.shard_map(
        functools.partial(local, mesh.shape["context"], mesh.shape["tensor"]),
        mesh=mesh,
        in_specs=placed,
        out_specs=P(("context", "tensor"), None),
        check_vma=False,
    )
```

```python
import functools
import math

import jax
import jax.numpy as jnp
import numpy as np
from jax import lax
from jax.experimental import pallas as pl
from jax.experimental.pallas import tpu as pltpu
from jax.sharding import PartitionSpec as P

HEAD = 128
BLOCK = 128
SLICE = 2 * BLOCK
NEGATIVE = -1e30
POSITIVE = 1e30
MESH = pl.DeviceIdType.MESH
F32 = jnp.float32
BF16 = jnp.bfloat16


LAYERS = ((0, 2 * BLOCK + 16), (2 * BLOCK + 16, 2 * BLOCK))
NUMBER = 2 * BLOCK
BIG = 2 * BLOCK + 16
SLOT = 4 * BLOCK + 16


def frequencies(width):
    counter = np.arange(width // 2, dtype=np.float32)
    inverse = np.float32(500000.0) ** (np.float32(-2.0) * counter / np.float32(width))
    wavelength = np.float32(2.0 * math.pi) / inverse
    smooth = np.clip((np.float32(8192.0) / wavelength - 1) / 3, 0, 1)
    f = (1 - smooth) * inverse / 8 + smooth * inverse
    return np.broadcast_to(np.concatenate([f, f])[None, :], (8, width)).astype(np.float32)


def dot_nn(a, b):
    return jnp.dot(a, b, preferred_element_type=F32)


def kernel(
    contexts, ranks, heads, block_rows,
    q_hbm, kv_hbm, place_hbm, freq_hbm, out_ref,
    queries, kv_ref, place_ref, freq_ref, landed, numbers, slab, staged, crossed,
    qq, keys_one, keys_two, vals_one, vals_two, vals_small, bias,
    out_big, out_small, max_big, max_small, part_out, part_in, sums_out, sums_in, done,
    in_sem, x_send, x_recv, z_send, z_recv, m_send, m_recv, r_send, r_recv, g_send, g_recv, p_send, p_recv, o_send, o_recv, k_sem,
):
    ring = contexts // 4
    group = SLICE // ranks
    half_groups = ranks // 2
    wide = min(4, ranks)
    deep = ranks // wide
    blocks = 2 * contexts
    scale = math.log2(math.e) / math.sqrt(HEAD)
    total = heads * BLOCK

    c = lax.axis_index("context")
    t = lax.axis_index("tensor")
    core = lax.rem(c, 2)
    y = lax.rem(lax.div(c, 2), ring)
    z = lax.div(c, 2 * ring)
    half_ring = ring // 2

    def at(zz, yy, cc):
        return (zz * ring + yy) * 2 + cc

    def turn(v):
        return lax.rem(v + 2 * ring, ring)

    after = at(z, turn(y + 1), core)
    before = at(z, turn(y + ring - 1), core)
    sibling = at(z, y, 1 - core)
    across = at(1 - z, y, core)
    x = lax.rem(t, wide)
    low_z = lax.div(t, wide)

    def row_peer(k):
        return low_z * wide + lax.rem(x + k, wide)

    def near_peer(k):
        return lax.rem(low_z + k, deep) * wide + x

    fetches = [
        pltpu.make_async_copy(src, dst, in_sem.at[i])
        for i, (src, dst) in enumerate((
            (place_hbm, place_ref), (freq_hbm, freq_ref), (kv_hbm, kv_ref), (q_hbm, queries)
        ))
    ]
    for fetch in fetches:
        fetch.start()

    barrier = pltpu.get_barrier_semaphore()

    def greet_group(k, carry):
        pl.semaphore_signal(
            barrier, inc=1, device_id=(c, lax.rem(t + k, ranks)), device_id_type=MESH
        )
        return carry

    def greet_far(k, carry):
        pl.semaphore_signal(
            barrier, inc=1, device_id=(across, near_peer(k)), device_id_type=MESH
        )
        return carry

    lax.fori_loop(1, ranks, greet_group, 0)
    lax.fori_loop(0, deep, greet_far, 0)
    for neighbour in (after, before, sibling):
        pl.semaphore_signal(barrier, inc=1, device_id=(neighbour, t), device_id_type=MESH)

    def number(half):
        return jnp.right_shift(place_ref[pl.ds(half, 1), :], 7).astype(F32)

    def rotation(block_number, start, rows):
        step = lax.broadcasted_iota(jnp.int32, (rows, HEAD), 0) + start
        angle = (block_number * BLOCK + step.astype(F32)) * freq_ref[0:1, :]
        lane = lax.broadcasted_iota(jnp.int32, (rows, HEAD), 1)
        return jnp.cos(angle), jnp.where(lane < HEAD // 2, -1.0, 1.0) * jnp.sin(angle)

    for fetch in fetches[:3]:
        fetch.wait()
    cos_k, sin_k = rotation(
        number(lax.div(t, half_groups)), lax.rem(t, half_groups) * group, group
    )
    for h in range(ranks // 2):
        cols = slice(h * HEAD, (h + 1) * HEAD)
        place = (h % (wide // 2), h // (wide // 2))
        value = kv_ref[0, :, cols].astype(F32)
        turned = value * cos_k + pltpu.roll(value, HEAD // 2, 1) * sin_k
        staged[place[0], place[1], 0] = turned.astype(BF16)
        staged[place[0], place[1], 1] = kv_ref[1, :, cols]
    numbers[z] = jnp.broadcast_to(number(0), (16, HEAD)).astype(BF16)

    pl.semaphore_wait(barrier, ranks - 1 + deep + 3)

    def row_copy(k):
        peer = row_peer(k)
        return pltpu.make_async_remote_copy(
            src_ref=staged.at[lax.div(lax.rem(peer, wide), 2)],
            dst_ref=crossed.at[x],
            send_sem=x_send.at[k],
            recv_sem=x_recv.at[x],
            device_id=(c, peer),
            device_id_type=MESH,
        )

    def row_wait(k):
        pltpu.make_async_remote_copy(
            src_ref=staged.at[0],
            dst_ref=crossed.at[lax.rem(x + k, wide)],
            send_sem=x_send.at[k],
            recv_sem=x_recv.at[lax.rem(x + k, wide)],
            device_id=(c, row_peer(k)),
            device_id_type=MESH,
        ).wait_recv()

    def column_copy(k, target, part):
        peer = near_peer(k)
        return pltpu.make_async_remote_copy(
            src_ref=crossed.at[:, lax.div(peer, wide)],
            dst_ref=landed.at[z, pl.ds(low_z * wide, wide)],
            send_sem=z_send.at[part, k],
            recv_sem=z_recv.at[z, low_z],
            device_id=(target, peer),
            device_id_type=MESH,
        )

    def column_wait(zz, k):
        source = lax.rem(low_z + k, deep)
        pltpu.make_async_remote_copy(
            src_ref=crossed.at[:, 0],
            dst_ref=landed.at[zz, pl.ds(source * wide, wide)],
            send_sem=z_send.at[0, 0],
            recv_sem=z_recv.at[zz, source],
            device_id=(across, t),
            device_id_type=MESH,
        ).wait_recv()

    def id_copy(zz):
        return pltpu.make_async_remote_copy(
            src_ref=numbers.at[zz],
            dst_ref=numbers.at[zz],
            send_sem=m_send.at[0],
            recv_sem=m_recv.at[0],
            device_id=(across, t),
            device_id_type=MESH,
        )

    for k in range(1, wide):
        row_copy(k).start()
    id_copy(z).start()
    crossed[x] = staged[lax.div(x, 2)]
    for k in range(1, wide):
        row_wait(k)
    for k in range(1, deep):
        column_copy(k, c, 0).start()
    for k in range(deep):
        column_copy(k, across, 1).start()
    landed[z, pl.ds(low_z * wide, wide)] = crossed[:, low_z]

    def slot(k, way, s):
        return at(lax.rem(z + s, 2), turn(y + ring - (1 - 2 * way) * k), core)

    def move(where, layer, send, recv, target):
        low, size = LAYERS[layer]
        view = slab.at[where, pl.ds(low, size)]
        return pltpu.make_async_remote_copy(
            src_ref=view, dst_ref=view, send_sem=send, recv_sem=recv,
            device_id=(target, t), device_id_type=MESH,
        )

    def entry(way, s, layer):
        return 4 * way + 2 * s + layer

    def ring_copy(k, way, s, layer):
        e = entry(way, s, layer)
        target = at(z, turn(y + ring + 1 - 2 * way), core)
        return move(
            slot(k, way, s), layer, r_send.at[k, e], r_recv.at[k + 1, e], target
        )

    def ring_wait(k, way, s, layer):
        e = entry(way, s, layer)
        move(
            slot(k, way, s), layer, r_send.at[k, e], r_recv.at[k, e], after
        ).wait_recv()

    def goes_on(k, way, s):
        return jnp.logical_or(k < half_ring - 1, jnp.logical_and(k == half_ring - 1, s == way))

    def arrive(k, s, layer):
        for way in range(2):

            @pl.when(goes_on(k - 1, way, s))
            def _():
                ring_wait(k, way, s, layer)

                @pl.when(goes_on(k, way, s))
                def _():
                    ring_copy(k, way, s, layer).start()

    def arrange(zz):
        where = at(zz, y, core)
        first = numbers[zz].astype(F32)[0:1, :]
        smaller = first < blocks / 2
        halves = []
        for plane_index in range(2):
            pair = []
            for i in range(2):
                pieces = [
                    landed[zz, i * half_groups + g, plane_index] for g in range(half_groups)
                ]
                pair.append(jnp.concatenate(pieces, axis=0).astype(F32))
            halves.append(jnp.where(smaller, pair[0], pair[1]))
            halves.append(jnp.where(smaller, pair[1], pair[0]))
        slab[where, 0:BLOCK] = halves[0].T.astype(BF16)
        slab[where, BLOCK:2 * BLOCK] = halves[2].astype(BF16)
        low = jnp.minimum(first, blocks - 1 - first)
        slab[where, NUMBER:NUMBER + 16] = jnp.broadcast_to(low, (16, HEAD)).astype(BF16)
        slab[where, BIG:BIG + BLOCK] = halves[1].T.astype(BF16)
        slab[where, BIG + BLOCK:SLOT] = halves[3].astype(BF16)

    def launch(s):
        for layer in range(2):
            for way in range(2):
                if half_ring > 1 or s == way:
                    ring_copy(0, way, s, layer).start()

    first_id = number(0)
    first_small = first_id < blocks / 2
    fetches[3].wait()
    turns = [rotation(number(i), 0, BLOCK) for i in range(2)]
    for h in range(heads):
        rows = slice(h * BLOCK, (h + 1) * BLOCK)
        turned = []
        for i in range(2):
            value = queries[i * BLOCK:(i + 1) * BLOCK, h * HEAD:(h + 1) * HEAD].astype(F32)
            turned.append(value * turns[i][0] + pltpu.roll(value, HEAD // 2, 1) * turns[i][1])
        qq[1, rows, 0:HEAD] = jnp.where(first_small, turned[0], turned[1]).astype(BF16)
        qq[1, rows, HEAD:2 * HEAD] = jnp.where(first_small, turned[1], turned[0]).astype(BF16)
    qq[1, total:total + 16, :] = jnp.broadcast_to(
        jnp.concatenate([first_id, first_id], axis=1), (16, 2 * HEAD)
    ).astype(BF16)
    swap = pltpu.make_async_remote_copy(
        src_ref=qq.at[1], dst_ref=qq.at[0], send_sem=g_send.at[0], recv_sem=g_recv.at[0],
        device_id=(sibling, t), device_id_type=MESH,
    )
    swap.start()

    for k in range(1, deep):
        column_wait(z, k)
    arrange(z)
    launch(0)

    for k in range(deep):
        column_wait(1 - z, k)
    id_copy(1 - z).wait_recv()
    arrange(1 - z)
    launch(1)

    for best in (max_small, max_big):
        best[0] = jnp.full((total, HEAD), NEGATIVE, F32)
    for sums in (out_small, out_big):
        sums[0] = jnp.zeros((total, 2 * HEAD), F32)
    ones = jnp.ones((BLOCK, HEAD), BF16)
    token = lax.broadcasted_iota(jnp.int32, (BLOCK, BLOCK), 0)
    key = lax.broadcasted_iota(jnp.int32, (BLOCK, BLOCK), 1)

    def diagonal(h, carry):
        rows = pl.ds(pl.multiple_of(h * BLOCK, BLOCK), BLOCK)
        for i, (best, sums) in enumerate(((max_small, out_small), (max_big, out_big))):
            s = dot_nn(qq[1, rows, i * HEAD:(i + 1) * HEAD], slab[c, i * BIG:i * BIG + BLOCK])
            s = jnp.where(key <= token, s, NEGATIVE)
            m = jnp.max(s, axis=1, keepdims=True)
            best[1, rows, :] = jnp.broadcast_to(m, (BLOCK, HEAD))
            values = jnp.concatenate(
                [slab[c, i * BIG + BLOCK:i * BIG + 2 * BLOCK], ones], axis=1
            )
            sums[1, rows, :] = dot_nn(jnp.exp2((s - m) * scale).astype(BF16), values)
        return carry

    lax.fori_loop(0, heads, diagonal, 0)
    for i in range(4):
        vals_one[i * BLOCK:(i + 1) * BLOCK, HEAD:2 * HEAD] = ones

    def flag(condition):
        return jnp.where(condition, 1.0, 0.0)

    def prepare(places, owner):
        asker = qq[owner, total:total + 16, 0:HEAD].astype(F32)[0:1, :]
        my_small = jnp.minimum(asker, blocks - 1 - asker)
        for i, where in enumerate(places):
            small = slab[where, NUMBER:NUMBER + 16].astype(F32)[0:1, :]
            low = flag(small < my_small)
            high = flag(small > my_small)
            bias[2 * i] = jnp.broadcast_to((high - 1.0) * POSITIVE, (8, HEAD))
            bias[2 * i + 1] = jnp.broadcast_to((low - 1.0) * POSITIVE, (8, HEAD))
            low = low.astype(BF16)
            high = high.astype(BF16)
            span = slice(i * BLOCK, (i + 1) * BLOCK)
            k_small = slab[where, 0:BLOCK]
            k_big = slab[where, BIG:BIG + BLOCK]
            v_small = slab[where, BLOCK:2 * BLOCK]
            v_big = slab[where, BIG + BLOCK:SLOT]
            keys_one[:, span] = k_small
            keys_two[0:HEAD, span] = k_small * low
            keys_two[HEAD:2 * HEAD, span] = k_big * high
            vals_one[span, 0:HEAD] = v_small
            vals_two[span, 0:HEAD] = v_big * high
            vals_two[span, HEAD:2 * HEAD] = ones * high
            vals_small[span, 0:HEAD] = v_small * low
            vals_small[span, HEAD:2 * HEAD] = ones * low

    def advance(n, owner, s):
        starts = range(s * half_rows, (s + 1) * half_rows, block_rows)
        keys = slice(0, n * BLOCK)
        bias_big = [bias[2 * i][0:1, :] for i in range(n)]
        bias_small = [bias[2 * i + 1][0:1, :] for i in range(n)]
        scores = []
        for start in starts:
            q = qq[owner, start:start + block_rows, :]
            scores.append((
                dot_nn(q[:, HEAD:2 * HEAD], keys_one[:, keys]), dot_nn(q, keys_two[:, keys])
            ))
        for start, (one, two) in zip(starts, scores):
            rows = slice(start, start + block_rows)
            ones_of = [one[:, i * BLOCK:(i + 1) * BLOCK] for i in range(n)]
            twos_of = [two[:, i * BLOCK:(i + 1) * BLOCK] for i in range(n)]
            big = functools.reduce(
                jnp.maximum, ones_of + [x + w for x, w in zip(twos_of, bias_big)]
            )
            small = functools.reduce(
                jnp.maximum, [x + w for x, w in zip(twos_of, bias_small)]
            )
            old_big = max_big[owner, rows, :]
            old_small = max_small[owner, rows, :]
            new_big = jnp.maximum(old_big, jnp.max(big, axis=1, keepdims=True))
            new_small = jnp.maximum(old_small, jnp.max(small, axis=1, keepdims=True))
            max_big[owner, rows, :] = new_big
            max_small[owner, rows, :] = new_small
            alpha_big = jnp.exp2((old_big - new_big) * scale)
            alpha_small = jnp.exp2((old_small - new_small) * scale)
            weights = [jnp.exp2((x - new_big) * scale).astype(BF16) for x in ones_of]
            later = []
            for x, wb, ws in zip(twos_of, bias_big, bias_small):
                m = jnp.where(wb == 0.0, new_big, jnp.where(ws == 0.0, new_small, POSITIVE))
                later.append(jnp.exp2((x - m) * scale).astype(BF16))
            later = jnp.concatenate(later, axis=1)
            every = jnp.concatenate(weights + [later], axis=1)
            values = jnp.concatenate([vals_one[keys, :], vals_two[keys, :]], axis=0)
            wide_big = jnp.concatenate([alpha_big, alpha_big], axis=1)
            wide_small = jnp.concatenate([alpha_small, alpha_small], axis=1)
            out_big[owner, rows, :] = out_big[owner, rows, :] * wide_big + dot_nn(every, values)
            out_small[owner, rows, :] = (
                out_small[owner, rows, :] * wide_small + dot_nn(later, vals_small[keys, :])
            )

    half_heads = heads // 2
    half_rows = total // 2

    lane = lax.broadcasted_iota(jnp.int32, (BLOCK, HEAD), 1)
    log2_e = math.log2(math.e)

    def log_sum(best, weight):
        return best * scale + jnp.log(weight) * log2_e

    def part_copy(i):
        if i == 2:
            src, dst = sums_out, sums_in
        else:
            src = part_out.at[pl.ds(i * half_rows, half_rows)]
            dst = part_in.at[pl.ds(i * half_rows, half_rows)]
        return pltpu.make_async_remote_copy(
            src_ref=src, dst_ref=dst, send_sem=p_send.at[i], recv_sem=p_recv.at[i],
            device_id=(sibling, t), device_id_type=MESH,
        )

    def give_back(s):
        packed = jnp.zeros((BLOCK, HEAD), F32) if s == 0 else sums_out[...]
        for h in range(s * half_heads, (s + 1) * half_heads):
            rows = slice(h * BLOCK, (h + 1) * BLOCK)
            for i, (best, sums) in enumerate(((max_small, out_small), (max_big, out_big))):
                weight = jnp.maximum(sums[0, rows, HEAD:2 * HEAD], 1.0)
                part_out[rows, i * HEAD:(i + 1) * HEAD] = (
                    sums[0, rows, 0:HEAD] / weight
                ).astype(BF16)
                first = h * 16 + i * 8
                inside = jnp.logical_and(lane >= first, lane < first + 8)
                packed = jnp.where(inside, log_sum(best[0, rows, :], weight), packed)
        sums_out[...] = packed
        part_copy(s).start()

    width = half_heads * HEAD

    def columns(rank, s):
        return pl.ds(pl.multiple_of((2 * rank + s) * width, width), width)

    def tokens(rank):
        return pl.ds(pl.multiple_of(rank * group, group), group)

    def out_move(src, dst, s, send, recv, target):
        return pltpu.make_async_remote_copy(
            src_ref=done.at[tokens(src), pl.ds(s * width, width)],
            dst_ref=out_ref.at[:, columns(dst, s)],
            send_sem=o_send.at[send, s],
            recv_sem=o_recv.at[recv, s],
            device_id=(c, target),
            device_id_type=MESH,
        )

    def out_keep(s):
        return pltpu.make_async_copy(
            done.at[tokens(t), pl.ds(s * width, width)], out_ref.at[:, columns(t, s)], k_sem.at[s]
        )

    def finish(s):
        for h in range(s * half_heads, (s + 1) * half_heads):
            rows = slice(h * BLOCK, (h + 1) * BLOCK)
            cols = slice(h * HEAD, (h + 1) * HEAD)
            merged = []
            for i, (best, sums) in enumerate(((max_small, out_small), (max_big, out_big))):
                weight = sums[1, rows, HEAD:2 * HEAD]
                mine = log_sum(best[1, rows, :], weight)
                first = h * 16 + i * 8
                theirs = jnp.broadcast_to(sums_in[:, first:first + 1], (BLOCK, HEAD))
                top = jnp.maximum(mine, theirs)
                mine = jnp.exp2(mine - top)
                theirs = jnp.exp2(theirs - top)
                other_part = part_in[rows, i * HEAD:(i + 1) * HEAD].astype(F32)
                value = sums[1, rows, 0:HEAD] * (mine / weight) + other_part * theirs
                merged.append(value / (mine + theirs))
            small, big = merged
            done[0:BLOCK, cols] = jnp.where(first_small, small, big).astype(BF16)
            done[BLOCK:SLICE, cols] = jnp.where(first_small, big, small).astype(BF16)

        def out_start(k, carry):
            pt = lax.rem(t + k, ranks)
            out_move(pt, t, s, pt, t, pt).start()
            return carry

        lax.fori_loop(1, ranks, out_start, 0)
        out_keep(s).start()

    def attend(k, ways, owner):
        prepare([slot(k, way, s) for way in ways for s in range(2)], owner)
        for s in range(2):
            advance(2 * len(ways), owner, s)
            arrive(k + 1, owner, s)

    swap.wait_recv()

    def first_step(owner, carry):
        attend(0, (0,), owner)
        return carry

    lax.fori_loop(0, 2, first_step, 0)

    def step(i, carry):
        attend(lax.div(i, 2) + 1, (0, 1), lax.rem(i, 2))
        return carry

    if half_ring > 1:
        lax.fori_loop(0, 2 * (half_ring - 1), step, 0)

    last = [slot(half_ring, 0, s) for s in range(2)]
    prepare(last, 0)
    for s in range(2):
        advance(2, 0, s)
        give_back(s)
    part_copy(2).start()
    prepare(last, 1)
    advance(2, 1, 0)
    part_copy(2).wait_recv()
    part_copy(0).wait_recv()
    finish(0)
    advance(2, 1, 1)
    part_copy(1).wait_recv()
    finish(1)

    def ring_sent(k, carry):
        for way in range(2):
            for s in range(2):
                for layer in range(2):

                    @pl.when(goes_on(k, way, s))
                    def _():
                        ring_copy(k, way, s, layer).wait_send()

        return carry

    def out_sent(k, carry):
        pt = lax.rem(t + k, ranks)
        for s in range(2):
            out_move(pt, t, s, pt, t, pt).wait_send()
        return carry

    def out_wait(k, carry):
        pt = lax.rem(t + k, ranks)
        for s in range(2):
            out_move(t, pt, s, t, pt, pt).wait_recv()
        return carry

    for k in range(1, wide):
        row_copy(k).wait_send()
    for k in range(1, deep):
        column_copy(k, c, 0).wait_send()
    for k in range(deep):
        column_copy(k, across, 1).wait_send()
    id_copy(z).wait_send()
    lax.fori_loop(0, half_ring, ring_sent, 0)
    swap.wait_send()
    for i in range(3):
        part_copy(i).wait_send()
    for s in range(2):
        out_keep(s).wait()
    lax.fori_loop(1, ranks, out_sent, 0)
    lax.fori_loop(1, ranks, out_wait, 0)


def local(contexts, ranks, queries, key_value_rows, positions):
    heads = queries.shape[1] // HEAD
    group = SLICE // ranks
    ring = contexts // 4
    wide = min(4, ranks)
    deep = ranks // wide
    rows = heads * BLOCK
    block_rows = min(256, rows // 4)
    dma = pltpu.SemaphoreType.DMA
    return pl.pallas_call(
        functools.partial(kernel, contexts, ranks, heads, block_rows),
        out_shape=jax.ShapeDtypeStruct((group, ranks * heads * HEAD), BF16),
        in_specs=[pl.BlockSpec(memory_space=pltpu.HBM)] * 4,
        out_specs=pl.BlockSpec(memory_space=pltpu.HBM),
        scratch_shapes=[
            pltpu.VMEM((SLICE, heads * HEAD), BF16),
            pltpu.VMEM((2, group, ranks // 2 * HEAD), BF16),
            pltpu.VMEM((2, BLOCK), jnp.int32),
            pltpu.VMEM((8, HEAD), F32),
            pltpu.VMEM((2, ranks, 2, group, HEAD), BF16),
            pltpu.VMEM((2, 16, HEAD), BF16),
            pltpu.VMEM((contexts, SLOT, HEAD), BF16),
            pltpu.VMEM((wide // 2, deep, 2, group, HEAD), BF16),
            pltpu.VMEM((wide, deep, 2, group, HEAD), BF16),
            pltpu.VMEM((2, rows + 16, 2 * HEAD), BF16),
            pltpu.VMEM((HEAD, 4 * BLOCK), BF16),
            pltpu.VMEM((2 * HEAD, 4 * BLOCK), BF16),
            pltpu.VMEM((4 * BLOCK, 2 * HEAD), BF16),
            pltpu.VMEM((4 * BLOCK, 2 * HEAD), BF16),
            pltpu.VMEM((4 * BLOCK, 2 * HEAD), BF16),
            pltpu.VMEM((8, 8, HEAD), F32),
            pltpu.VMEM((2, rows, 2 * HEAD), F32),
            pltpu.VMEM((2, rows, 2 * HEAD), F32),
            pltpu.VMEM((2, rows, HEAD), F32),
            pltpu.VMEM((2, rows, HEAD), F32),
            pltpu.VMEM((rows, 2 * HEAD), BF16),
            pltpu.VMEM((rows, 2 * HEAD), BF16),
            pltpu.VMEM((BLOCK, HEAD), F32),
            pltpu.VMEM((BLOCK, HEAD), F32),
            pltpu.VMEM((SLICE, heads * HEAD), BF16),
            dma((4,)),
            dma((wide,)),
            dma((wide,)),
            dma((2, deep)),
            dma((2, deep)),
            dma((1,)),
            dma((1,)),
            dma((ring // 2 + 1, 8)),
            dma((ring // 2 + 1, 8)),
            dma((1,)),
            dma((1,)),
            dma((3,)),
            dma((3,)),
            dma((ranks, 2)),
            dma((ranks, 2)),
            dma((2,)),
        ],
        compiler_params=pltpu.CompilerParams(
            collective_id=0, has_side_effects=True, vmem_limit_bytes=60 * 1024 * 1024
        ),
        cost_estimate=pl.CostEstimate(
            flops=8 * rows * SLICE * contexts * HEAD // 2,
            bytes_accessed=4 * 1024 * 1024,
            transcendentals=rows * SLICE * contexts,
        ),
    )(queries, key_value_rows, positions.reshape(2, BLOCK), jnp.asarray(frequencies(HEAD)))


def solution(mesh):
    placed = (P("context", "tensor"), P(None, ("context", "tensor"), None), P("context"))
    return jax.shard_map(
        functools.partial(local, mesh.shape["context"], mesh.shape["tensor"]),
        mesh=mesh,
        in_specs=placed,
        out_specs=P(("context", "tensor"), None),
        check_vma=False,
    )
```

```python
import functools
import math

import jax
import jax.numpy as jnp
import numpy as np
from jax import lax
from jax.experimental import pallas as pl
from jax.experimental.pallas import tpu as pltpu
from jax.sharding import PartitionSpec as P

HEAD = 128
BLOCK = 128
SLICE = 2 * BLOCK
NEGATIVE = -1e30
POSITIVE = 1e30
MESH = pl.DeviceIdType.MESH
F32 = jnp.float32
BF16 = jnp.bfloat16


LAYERS = ((0, 2 * BLOCK + 16), (2 * BLOCK + 16, 2 * BLOCK))
NUMBER = 2 * BLOCK
BIG = 2 * BLOCK + 16
SLOT = 4 * BLOCK + 16


def frequencies(width):
    counter = np.arange(width // 2, dtype=np.float32)
    inverse = np.float32(500000.0) ** (np.float32(-2.0) * counter / np.float32(width))
    wavelength = np.float32(2.0 * math.pi) / inverse
    smooth = np.clip((np.float32(8192.0) / wavelength - 1) / 3, 0, 1)
    f = (1 - smooth) * inverse / 8 + smooth * inverse
    return np.broadcast_to(np.concatenate([f, f])[None, :], (8, width)).astype(np.float32)


def dot_nn(a, b):
    return jnp.dot(a, b, preferred_element_type=F32)


def kernel(
    contexts, ranks, heads, block_rows,
    q_hbm, kv_hbm, place_hbm, freq_hbm, out_ref,
    queries, kv_ref, place_ref, freq_ref, landed, numbers, slab, staged, crossed,
    qq, keys_one, keys_two, vals_one, vals_two, vals_small, bias,
    out_big, out_small, max_big, max_small, part_out, part_in, sums_out, sums_in, done,
    in_sem, x_send, x_recv, z_send, z_recv, m_send, m_recv, r_send, r_recv, g_send, g_recv, p_send, p_recv, o_send, o_recv, k_sem,
):
    ring = contexts // 4
    group = SLICE // ranks
    half_groups = ranks // 2
    wide = min(4, ranks)
    deep = ranks // wide
    blocks = 2 * contexts
    scale = math.log2(math.e) / math.sqrt(HEAD)
    total = heads * BLOCK

    c = lax.axis_index("context")
    t = lax.axis_index("tensor")
    core = lax.rem(c, 2)
    y = lax.rem(lax.div(c, 2), ring)
    z = lax.div(c, 2 * ring)
    half_ring = ring // 2

    def at(zz, yy, cc):
        return (zz * ring + yy) * 2 + cc

    def turn(v):
        return lax.rem(v + 2 * ring, ring)

    after = at(z, turn(y + 1), core)
    before = at(z, turn(y + ring - 1), core)
    sibling = at(z, y, 1 - core)
    across = at(1 - z, y, core)
    x = lax.rem(t, wide)
    low_z = lax.div(t, wide)

    def row_peer(k):
        return low_z * wide + lax.rem(x + k, wide)

    def near_peer(k):
        return lax.rem(low_z + k, deep) * wide + x

    fetches = [
        pltpu.make_async_copy(src, dst, in_sem.at[i])
        for i, (src, dst) in enumerate((
            (place_hbm, place_ref), (freq_hbm, freq_ref), (kv_hbm, kv_ref), (q_hbm, queries)
        ))
    ]
    for fetch in fetches:
        fetch.start()

    barrier = pltpu.get_barrier_semaphore()

    def greet_group(k, carry):
        pl.semaphore_signal(
            barrier, inc=1, device_id=(c, lax.rem(t + k, ranks)), device_id_type=MESH
        )
        return carry

    def greet_far(k, carry):
        pl.semaphore_signal(
            barrier, inc=1, device_id=(across, near_peer(k)), device_id_type=MESH
        )
        return carry

    lax.fori_loop(1, ranks, greet_group, 0)
    lax.fori_loop(0, deep, greet_far, 0)
    for neighbour in (after, before, sibling):
        pl.semaphore_signal(barrier, inc=1, device_id=(neighbour, t), device_id_type=MESH)

    def number(half):
        return jnp.right_shift(place_ref[pl.ds(half, 1), :], 7).astype(F32)

    def rotation(block_number, start, rows):
        step = lax.broadcasted_iota(jnp.int32, (rows, HEAD), 0) + start
        angle = (block_number * BLOCK + step.astype(F32)) * freq_ref[0:1, :]
        lane = lax.broadcasted_iota(jnp.int32, (rows, HEAD), 1)
        return jnp.cos(angle), jnp.where(lane < HEAD // 2, -1.0, 1.0) * jnp.sin(angle)

    for fetch in fetches[:3]:
        fetch.wait()
    cos_k, sin_k = rotation(
        number(lax.div(t, half_groups)), lax.rem(t, half_groups) * group, group
    )
    for h in range(ranks // 2):
        cols = slice(h * HEAD, (h + 1) * HEAD)
        place = (h % (wide // 2), h // (wide // 2))
        value = kv_ref[0, :, cols].astype(F32)
        turned = value * cos_k + pltpu.roll(value, HEAD // 2, 1) * sin_k
        staged[place[0], place[1], 0] = turned.astype(BF16)
        staged[place[0], place[1], 1] = kv_ref[1, :, cols]
    numbers[z] = jnp.broadcast_to(number(0), (16, HEAD)).astype(BF16)

    pl.semaphore_wait(barrier, ranks - 1 + deep + 3)

    def row_copy(k):
        peer = row_peer(k)
        return pltpu.make_async_remote_copy(
            src_ref=staged.at[lax.div(lax.rem(peer, wide), 2)],
            dst_ref=crossed.at[x],
            send_sem=x_send.at[k],
            recv_sem=x_recv.at[x],
            device_id=(c, peer),
            device_id_type=MESH,
        )

    def row_wait(k):
        pltpu.make_async_remote_copy(
            src_ref=staged.at[0],
            dst_ref=crossed.at[lax.rem(x + k, wide)],
            send_sem=x_send.at[k],
            recv_sem=x_recv.at[lax.rem(x + k, wide)],
            device_id=(c, row_peer(k)),
            device_id_type=MESH,
        ).wait_recv()

    def column_copy(k, target, part):
        peer = near_peer(k)
        return pltpu.make_async_remote_copy(
            src_ref=crossed.at[:, lax.div(peer, wide)],
            dst_ref=landed.at[z, pl.ds(low_z * wide, wide)],
            send_sem=z_send.at[part, k],
            recv_sem=z_recv.at[z, low_z],
            device_id=(target, peer),
            device_id_type=MESH,
        )

    def column_wait(zz, k):
        source = lax.rem(low_z + k, deep)
        pltpu.make_async_remote_copy(
            src_ref=crossed.at[:, 0],
            dst_ref=landed.at[zz, pl.ds(source * wide, wide)],
            send_sem=z_send.at[0, 0],
            recv_sem=z_recv.at[zz, source],
            device_id=(across, t),
            device_id_type=MESH,
        ).wait_recv()

    def id_copy(zz):
        return pltpu.make_async_remote_copy(
            src_ref=numbers.at[zz],
            dst_ref=numbers.at[zz],
            send_sem=m_send.at[0],
            recv_sem=m_recv.at[0],
            device_id=(across, t),
            device_id_type=MESH,
        )

    for k in range(1, wide):
        row_copy(k).start()
    id_copy(z).start()
    crossed[x] = staged[lax.div(x, 2)]
    for k in range(1, wide):
        row_wait(k)
    for k in range(1, deep):
        column_copy(k, c, 0).start()
    for k in range(deep):
        column_copy(k, across, 1).start()
    landed[z, pl.ds(low_z * wide, wide)] = crossed[:, low_z]

    def slot(k, way, s):
        return at(lax.rem(z + s, 2), turn(y + ring - (1 - 2 * way) * k), core)

    def move(where, layer, send, recv, target):
        low, size = LAYERS[layer]
        view = slab.at[where, pl.ds(low, size)]
        return pltpu.make_async_remote_copy(
            src_ref=view, dst_ref=view, send_sem=send, recv_sem=recv,
            device_id=(target, t), device_id_type=MESH,
        )

    def entry(way, s, layer):
        return 4 * way + 2 * s + layer

    def ring_copy(k, way, s, layer):
        e = entry(way, s, layer)
        target = at(z, turn(y + ring + 1 - 2 * way), core)
        return move(
            slot(k, way, s), layer, r_send.at[k, e], r_recv.at[k + 1, e], target
        )

    def ring_wait(k, way, s, layer):
        e = entry(way, s, layer)
        move(
            slot(k, way, s), layer, r_send.at[k, e], r_recv.at[k, e], after
        ).wait_recv()

    def goes_on(k, way, s):
        return jnp.logical_or(k < half_ring - 1, jnp.logical_and(k == half_ring - 1, s == way))

    def arrive(k, s, layer):
        for way in range(2):

            @pl.when(goes_on(k - 1, way, s))
            def _():
                ring_wait(k, way, s, layer)

                @pl.when(goes_on(k, way, s))
                def _():
                    ring_copy(k, way, s, layer).start()

    def arrange(zz):
        where = at(zz, y, core)
        first = numbers[zz].astype(F32)[0:1, :]
        smaller = first < blocks / 2
        halves = []
        for plane_index in range(2):
            pair = []
            for i in range(2):
                pieces = [
                    landed[zz, i * half_groups + g, plane_index] for g in range(half_groups)
                ]
                pair.append(jnp.concatenate(pieces, axis=0).astype(F32))
            halves.append(jnp.where(smaller, pair[0], pair[1]))
            halves.append(jnp.where(smaller, pair[1], pair[0]))
        slab[where, 0:BLOCK] = halves[0].T.astype(BF16)
        slab[where, BLOCK:2 * BLOCK] = halves[2].astype(BF16)
        low = jnp.minimum(first, blocks - 1 - first)
        slab[where, NUMBER:NUMBER + 16] = jnp.broadcast_to(low, (16, HEAD)).astype(BF16)
        slab[where, BIG:BIG + BLOCK] = halves[1].T.astype(BF16)
        slab[where, BIG + BLOCK:SLOT] = halves[3].astype(BF16)

    def launch(s):
        for layer in range(2):
            for way in range(2):
                if half_ring > 1 or s == way:
                    ring_copy(0, way, s, layer).start()

    first_id = number(0)
    first_small = first_id < blocks / 2
    fetches[3].wait()
    turns = [rotation(number(i), 0, BLOCK) for i in range(2)]
    for h in range(heads):
        rows = slice(h * BLOCK, (h + 1) * BLOCK)
        turned = []
        for i in range(2):
            value = queries[i * BLOCK:(i + 1) * BLOCK, h * HEAD:(h + 1) * HEAD].astype(F32)
            turned.append(value * turns[i][0] + pltpu.roll(value, HEAD // 2, 1) * turns[i][1])
        qq[1, rows, 0:HEAD] = jnp.where(first_small, turned[0], turned[1]).astype(BF16)
        qq[1, rows, HEAD:2 * HEAD] = jnp.where(first_small, turned[1], turned[0]).astype(BF16)
    qq[1, total:total + 16, :] = jnp.broadcast_to(
        jnp.concatenate([first_id, first_id], axis=1), (16, 2 * HEAD)
    ).astype(BF16)
    swap = pltpu.make_async_remote_copy(
        src_ref=qq.at[1], dst_ref=qq.at[0], send_sem=g_send.at[0], recv_sem=g_recv.at[0],
        device_id=(sibling, t), device_id_type=MESH,
    )
    swap.start()

    for k in range(1, deep):
        column_wait(z, k)
    arrange(z)
    launch(0)

    for k in range(deep):
        column_wait(1 - z, k)
    id_copy(1 - z).wait_recv()
    arrange(1 - z)
    launch(1)

    for best in (max_small, max_big):
        best[0] = jnp.full((total, HEAD), NEGATIVE, F32)
    for sums in (out_small, out_big):
        sums[0] = jnp.zeros((total, 2 * HEAD), F32)
    ones = jnp.ones((BLOCK, HEAD), BF16)
    token = lax.broadcasted_iota(jnp.int32, (BLOCK, BLOCK), 0)
    key = lax.broadcasted_iota(jnp.int32, (BLOCK, BLOCK), 1)

    def diagonal(h, carry):
        rows = pl.ds(pl.multiple_of(h * BLOCK, BLOCK), BLOCK)
        for i, (best, sums) in enumerate(((max_small, out_small), (max_big, out_big))):
            s = dot_nn(qq[1, rows, i * HEAD:(i + 1) * HEAD], slab[c, i * BIG:i * BIG + BLOCK])
            s = jnp.where(key <= token, s, NEGATIVE)
            m = jnp.max(s, axis=1, keepdims=True)
            best[1, rows, :] = jnp.broadcast_to(m, (BLOCK, HEAD))
            values = jnp.concatenate(
                [slab[c, i * BIG + BLOCK:i * BIG + 2 * BLOCK], ones], axis=1
            )
            sums[1, rows, :] = dot_nn(jnp.exp2((s - m) * scale).astype(BF16), values)
        return carry

    lax.fori_loop(0, heads, diagonal, 0)
    for i in range(4):
        vals_one[i * BLOCK:(i + 1) * BLOCK, HEAD:2 * HEAD] = ones

    def flag(condition):
        return jnp.where(condition, 1.0, 0.0)

    def prepare(places, owner):
        asker = qq[owner, total:total + 16, 0:HEAD].astype(F32)[0:1, :]
        my_small = jnp.minimum(asker, blocks - 1 - asker)
        for i, where in enumerate(places):
            small = slab[where, NUMBER:NUMBER + 16].astype(F32)[0:1, :]
            low = flag(small < my_small)
            high = flag(small > my_small)
            bias[2 * i] = jnp.broadcast_to((high - 1.0) * POSITIVE, (8, HEAD))
            bias[2 * i + 1] = jnp.broadcast_to((low - 1.0) * POSITIVE, (8, HEAD))
            low = low.astype(BF16)
            high = high.astype(BF16)
            span = slice(i * BLOCK, (i + 1) * BLOCK)
            k_small = slab[where, 0:BLOCK]
            k_big = slab[where, BIG:BIG + BLOCK]
            v_small = slab[where, BLOCK:2 * BLOCK]
            v_big = slab[where, BIG + BLOCK:SLOT]
            keys_one[:, span] = k_small
            keys_two[0:HEAD, span] = k_small * low
            keys_two[HEAD:2 * HEAD, span] = k_big * high
            vals_one[span, 0:HEAD] = v_small
            vals_two[span, 0:HEAD] = v_big * high
            vals_two[span, HEAD:2 * HEAD] = ones * high
            vals_small[span, 0:HEAD] = v_small * low
            vals_small[span, HEAD:2 * HEAD] = ones * low

    def advance(n, owner, own_slice, after_block):
        keys = slice(0, n * BLOCK)
        wide_piece = 2 * BLOCK
        pieces = range(n // 2)
        bias_big = [bias[2 * i][0:1, :] for i in range(n)]
        bias_small = [bias[2 * i + 1][0:1, :] for i in range(n)]
        starts = list(range(0, total, block_rows))

        def split(products):
            return [p[:, i * BLOCK:(i + 1) * BLOCK] for p in products for i in range(2)]

        def score_piece(start, p):
            q = qq[owner, start:start + block_rows, :]
            span = slice(p * wide_piece, (p + 1) * wide_piece)
            return dot_nn(q[:, HEAD:2 * HEAD], keys_one[:, span]), dot_nn(q, keys_two[:, span])

        def maxima(start, scores):
            rows = slice(start, start + block_rows)
            ones_of = split([one for one, two in scores])
            twos_of = split([two for one, two in scores])
            big = functools.reduce(
                jnp.maximum, ones_of + [v + w for v, w in zip(twos_of, bias_big)]
            )
            small = functools.reduce(
                jnp.maximum, [v + w for v, w in zip(twos_of, bias_small)]
            )
            old_big = max_big[owner, rows, :]
            old_small = max_small[owner, rows, :]
            new_big = jnp.maximum(old_big, jnp.max(big, axis=1, keepdims=True))
            new_small = jnp.maximum(old_small, jnp.max(small, axis=1, keepdims=True))
            max_big[owner, rows, :] = new_big
            max_small[owner, rows, :] = new_small
            alpha_big = jnp.exp2((old_big - new_big) * scale)
            alpha_small = jnp.exp2((old_small - new_small) * scale)
            return ones_of, twos_of, new_big, new_small, alpha_big, alpha_small

        def weigh(state, p):
            ones_of, twos_of, new_big, new_small, alpha_big, alpha_small = state
            first, second = [], []
            for i in (2 * p, 2 * p + 1):
                first.append(jnp.exp2((ones_of[i] - new_big) * scale).astype(BF16))
                m = new_small
                if own_slice:
                    m = jnp.where(bias_small[i] == 0.0, new_small, POSITIVE)
                m = jnp.where(bias_big[i] == 0.0, new_big, m)
                second.append(jnp.exp2((twos_of[i] - m) * scale).astype(BF16))
            return first, second

        state = maxima(starts[0], [score_piece(starts[0], p) for p in pieces])
        for b, start in enumerate(starts):
            rows = slice(start, start + block_rows)
            following_scores, first, second = [], [], []
            for p in pieces:
                if b + 1 < len(starts):
                    following_scores.append(score_piece(starts[b + 1], p))
                one, two = weigh(state, p)
                first += one
                second += two
            later = jnp.concatenate(second, axis=1)
            every = jnp.concatenate(first + second, axis=1)
            values = jnp.concatenate([vals_one[keys, :], vals_two[keys, :]], axis=0)
            add_big = dot_nn(every, values)
            add_small = dot_nn(later, vals_small[keys, :])
            alpha_big, alpha_small = state[4], state[5]
            if b + 1 < len(starts):
                state = maxima(starts[b + 1], following_scores)
            wide_big = jnp.concatenate([alpha_big, alpha_big], axis=1)
            wide_small = jnp.concatenate([alpha_small, alpha_small], axis=1)
            out_big[owner, rows, :] = out_big[owner, rows, :] * wide_big + add_big
            out_small[owner, rows, :] = out_small[owner, rows, :] * wide_small + add_small
            after_block(b)

    half_heads = heads // 2
    half_rows = total // 2

    lane = lax.broadcasted_iota(jnp.int32, (BLOCK, HEAD), 1)
    log2_e = math.log2(math.e)

    def log_sum(best, weight):
        return best * scale + jnp.log(weight) * log2_e

    def part_copy(i):
        if i == 2:
            src, dst = sums_out, sums_in
        else:
            src = part_out.at[pl.ds(i * half_rows, half_rows)]
            dst = part_in.at[pl.ds(i * half_rows, half_rows)]
        return pltpu.make_async_remote_copy(
            src_ref=src, dst_ref=dst, send_sem=p_send.at[i], recv_sem=p_recv.at[i],
            device_id=(sibling, t), device_id_type=MESH,
        )

    def give_back(s):
        packed = jnp.zeros((BLOCK, HEAD), F32) if s == 0 else sums_out[...]
        for h in range(s * half_heads, (s + 1) * half_heads):
            rows = slice(h * BLOCK, (h + 1) * BLOCK)
            for i, (best, sums) in enumerate(((max_small, out_small), (max_big, out_big))):
                weight = jnp.maximum(sums[0, rows, HEAD:2 * HEAD], 1.0)
                part_out[rows, i * HEAD:(i + 1) * HEAD] = (
                    sums[0, rows, 0:HEAD] / weight
                ).astype(BF16)
                first = h * 16 + i * 8
                inside = jnp.logical_and(lane >= first, lane < first + 8)
                packed = jnp.where(inside, log_sum(best[0, rows, :], weight), packed)
        sums_out[...] = packed
        part_copy(s).start()

    width = half_heads * HEAD

    def columns(rank, s):
        return pl.ds(pl.multiple_of((2 * rank + s) * width, width), width)

    def tokens(rank):
        return pl.ds(pl.multiple_of(rank * group, group), group)

    def out_move(src, dst, s, send, recv, target):
        return pltpu.make_async_remote_copy(
            src_ref=done.at[tokens(src), pl.ds(s * width, width)],
            dst_ref=out_ref.at[:, columns(dst, s)],
            send_sem=o_send.at[send, s],
            recv_sem=o_recv.at[recv, s],
            device_id=(c, target),
            device_id_type=MESH,
        )

    def out_keep(s):
        return pltpu.make_async_copy(
            done.at[tokens(t), pl.ds(s * width, width)], out_ref.at[:, columns(t, s)], k_sem.at[s]
        )

    def finish(s):
        for h in range(s * half_heads, (s + 1) * half_heads):
            rows = slice(h * BLOCK, (h + 1) * BLOCK)
            cols = slice(h * HEAD, (h + 1) * HEAD)
            merged = []
            for i, (best, sums) in enumerate(((max_small, out_small), (max_big, out_big))):
                weight = sums[1, rows, HEAD:2 * HEAD]
                mine = log_sum(best[1, rows, :], weight)
                first = h * 16 + i * 8
                theirs = jnp.broadcast_to(sums_in[:, first:first + 1], (BLOCK, HEAD))
                top = jnp.maximum(mine, theirs)
                mine = jnp.exp2(mine - top)
                theirs = jnp.exp2(theirs - top)
                other_part = part_in[rows, i * HEAD:(i + 1) * HEAD].astype(F32)
                value = sums[1, rows, 0:HEAD] * (mine / weight) + other_part * theirs
                merged.append(value / (mine + theirs))
            small, big = merged
            done[0:BLOCK, cols] = jnp.where(first_small, small, big).astype(BF16)
            done[BLOCK:SLICE, cols] = jnp.where(first_small, big, small).astype(BF16)

        def out_start(k, carry):
            pt = lax.rem(t + k, ranks)
            out_move(pt, t, s, pt, t, pt).start()
            return carry

        lax.fori_loop(1, ranks, out_start, 0)
        out_keep(s).start()

    middle = total // block_rows // 2 - 1
    final = total // block_rows - 1
    swap.wait_recv()

    def first_step(owner, carry):
        prepare([slot(0, 0, s) for s in range(2)], owner)
        advance(2, owner, True, lambda b: None)
        return carry

    lax.fori_loop(0, 2, first_step, 0)
    for s in range(2):
        for layer in range(2):
            arrive(1, s, layer)

    def step(i, carry):
        k = lax.div(i, 2) + 1
        owner = lax.rem(i, 2)
        prepare([slot(k, way, s) for way in range(2) for s in range(2)], owner)

        def after_block(b):
            if b == middle:
                arrive(k + 1, owner, 0)
            if b == final:
                arrive(k + 1, owner, 1)

        advance(4, owner, False, after_block)
        return carry

    if half_ring > 1:
        lax.fori_loop(0, 2 * (half_ring - 1), step, 0)

    def return_block(b):
        if b == middle:
            give_back(0)
        if b == final:
            give_back(1)
            part_copy(2).start()

    def merge_block(b):
        if b == middle:
            part_copy(2).wait_recv()
            part_copy(0).wait_recv()
            finish(0)
        if b == final:
            part_copy(1).wait_recv()
            finish(1)

    last = [slot(half_ring, 0, s) for s in range(2)]
    prepare(last, 0)
    advance(2, 0, False, return_block)
    prepare(last, 1)
    advance(2, 1, False, merge_block)

    def ring_sent(k, carry):
        for way in range(2):
            for s in range(2):
                for layer in range(2):

                    @pl.when(goes_on(k, way, s))
                    def _():
                        ring_copy(k, way, s, layer).wait_send()

        return carry

    def out_sent(k, carry):
        pt = lax.rem(t + k, ranks)
        for s in range(2):
            out_move(pt, t, s, pt, t, pt).wait_send()
        return carry

    def out_wait(k, carry):
        pt = lax.rem(t + k, ranks)
        for s in range(2):
            out_move(t, pt, s, t, pt, pt).wait_recv()
        return carry

    for k in range(1, wide):
        row_copy(k).wait_send()
    for k in range(1, deep):
        column_copy(k, c, 0).wait_send()
    for k in range(deep):
        column_copy(k, across, 1).wait_send()
    id_copy(z).wait_send()
    lax.fori_loop(0, half_ring, ring_sent, 0)
    swap.wait_send()
    for i in range(3):
        part_copy(i).wait_send()
    for s in range(2):
        out_keep(s).wait()
    lax.fori_loop(1, ranks, out_sent, 0)
    lax.fori_loop(1, ranks, out_wait, 0)


def local(contexts, ranks, queries, key_value_rows, positions):
    heads = queries.shape[1] // HEAD
    group = SLICE // ranks
    ring = contexts // 4
    wide = min(4, ranks)
    deep = ranks // wide
    rows = heads * BLOCK
    block_rows = min(256, rows // 4)
    dma = pltpu.SemaphoreType.DMA
    return pl.pallas_call(
        functools.partial(kernel, contexts, ranks, heads, block_rows),
        out_shape=jax.ShapeDtypeStruct((group, ranks * heads * HEAD), BF16),
        in_specs=[pl.BlockSpec(memory_space=pltpu.HBM)] * 4,
        out_specs=pl.BlockSpec(memory_space=pltpu.HBM),
        scratch_shapes=[
            pltpu.VMEM((SLICE, heads * HEAD), BF16),
            pltpu.VMEM((2, group, ranks // 2 * HEAD), BF16),
            pltpu.VMEM((2, BLOCK), jnp.int32),
            pltpu.VMEM((8, HEAD), F32),
            pltpu.VMEM((2, ranks, 2, group, HEAD), BF16),
            pltpu.VMEM((2, 16, HEAD), BF16),
            pltpu.VMEM((contexts, SLOT, HEAD), BF16),
            pltpu.VMEM((wide // 2, deep, 2, group, HEAD), BF16),
            pltpu.VMEM((wide, deep, 2, group, HEAD), BF16),
            pltpu.VMEM((2, rows + 16, 2 * HEAD), BF16),
            pltpu.VMEM((HEAD, 4 * BLOCK), BF16),
            pltpu.VMEM((2 * HEAD, 4 * BLOCK), BF16),
            pltpu.VMEM((4 * BLOCK, 2 * HEAD), BF16),
            pltpu.VMEM((4 * BLOCK, 2 * HEAD), BF16),
            pltpu.VMEM((4 * BLOCK, 2 * HEAD), BF16),
            pltpu.VMEM((8, 8, HEAD), F32),
            pltpu.VMEM((2, rows, 2 * HEAD), F32),
            pltpu.VMEM((2, rows, 2 * HEAD), F32),
            pltpu.VMEM((2, rows, HEAD), F32),
            pltpu.VMEM((2, rows, HEAD), F32),
            pltpu.VMEM((rows, 2 * HEAD), BF16),
            pltpu.VMEM((rows, 2 * HEAD), BF16),
            pltpu.VMEM((BLOCK, HEAD), F32),
            pltpu.VMEM((BLOCK, HEAD), F32),
            pltpu.VMEM((SLICE, heads * HEAD), BF16),
            dma((4,)),
            dma((wide,)),
            dma((wide,)),
            dma((2, deep)),
            dma((2, deep)),
            dma((1,)),
            dma((1,)),
            dma((ring // 2 + 1, 8)),
            dma((ring // 2 + 1, 8)),
            dma((1,)),
            dma((1,)),
            dma((3,)),
            dma((3,)),
            dma((ranks, 2)),
            dma((ranks, 2)),
            dma((2,)),
        ],
        compiler_params=pltpu.CompilerParams(
            collective_id=0, has_side_effects=True, vmem_limit_bytes=60 * 1024 * 1024
        ),
        cost_estimate=pl.CostEstimate(
            flops=8 * rows * SLICE * contexts * HEAD // 2,
            bytes_accessed=4 * 1024 * 1024,
            transcendentals=rows * SLICE * contexts,
        ),
    )(queries, key_value_rows, positions.reshape(2, BLOCK), jnp.asarray(frequencies(HEAD)))


def solution(mesh):
    placed = (P("context", "tensor"), P(None, ("context", "tensor"), None), P("context"))
    return jax.shard_map(
        functools.partial(local, mesh.shape["context"], mesh.shape["tensor"]),
        mesh=mesh,
        in_specs=placed,
        out_specs=P(("context", "tensor"), None),
        check_vma=False,
    )
```

```python
import functools
import math

import jax
import jax.numpy as jnp
import numpy as np
from jax import lax
from jax.experimental import pallas as pl
from jax.experimental.pallas import tpu as pltpu
from jax.sharding import PartitionSpec as P

HEAD = 128
BLOCK = 128
SLICE = 2 * BLOCK
NEGATIVE = -1e30
POSITIVE = 1e30
MESH = pl.DeviceIdType.MESH
F32 = jnp.float32
BF16 = jnp.bfloat16


LAYERS = ((0, 2 * BLOCK + 16), (2 * BLOCK + 16, 2 * BLOCK))
NUMBER = 2 * BLOCK
BIG = 2 * BLOCK + 16
SLOT = 4 * BLOCK + 16


def frequencies(width):
    counter = np.arange(width // 2, dtype=np.float32)
    inverse = np.float32(500000.0) ** (np.float32(-2.0) * counter / np.float32(width))
    wavelength = np.float32(2.0 * math.pi) / inverse
    smooth = np.clip((np.float32(8192.0) / wavelength - 1) / 3, 0, 1)
    f = (1 - smooth) * inverse / 8 + smooth * inverse
    return np.broadcast_to(np.concatenate([f, f])[None, :], (8, width)).astype(np.float32)


def dot_nn(a, b):
    return jnp.dot(a, b, preferred_element_type=F32)


def kernel(
    contexts, ranks, heads, block_rows,
    q_hbm, kv_hbm, place_hbm, freq_hbm, out_ref,
    queries, kv_ref, place_ref, freq_ref, landed, numbers, slab, staged, crossed,
    qq, keys_one, keys_two, vals_one, vals_two, vals_small, bias,
    out_big, out_small, max_big, max_small, part_out, part_in, sums_out, sums_in, done,
    in_sem, x_send, x_recv, z_send, z_recv, m_send, m_recv, r_send, r_recv, g_send, g_recv, p_send, p_recv, o_send, o_recv, k_sem,
):
    ring = contexts // 4
    group = SLICE // ranks
    half_groups = ranks // 2
    wide = min(4, ranks)
    deep = ranks // wide
    blocks = 2 * contexts
    scale = math.log2(math.e) / math.sqrt(HEAD)
    total = heads * BLOCK

    c = lax.axis_index("context")
    t = lax.axis_index("tensor")
    core = lax.rem(c, 2)
    y = lax.rem(lax.div(c, 2), ring)
    z = lax.div(c, 2 * ring)
    half_ring = ring // 2

    def at(zz, yy, cc):
        return (zz * ring + yy) * 2 + cc

    def turn(v):
        return lax.rem(v + 2 * ring, ring)

    after = at(z, turn(y + 1), core)
    before = at(z, turn(y + ring - 1), core)
    sibling = at(z, y, 1 - core)
    across = at(1 - z, y, core)
    x = lax.rem(t, wide)
    low_z = lax.div(t, wide)

    def row_peer(k):
        return low_z * wide + lax.rem(x + k, wide)

    def near_peer(k):
        return lax.rem(low_z + k, deep) * wide + x

    fetches = [
        pltpu.make_async_copy(src, dst, in_sem.at[i])
        for i, (src, dst) in enumerate((
            (place_hbm, place_ref), (freq_hbm, freq_ref), (kv_hbm, kv_ref), (q_hbm, queries)
        ))
    ]
    for fetch in fetches:
        fetch.start()

    barrier = pltpu.get_barrier_semaphore()

    def greet_group(k, carry):
        pl.semaphore_signal(
            barrier, inc=1, device_id=(c, lax.rem(t + k, ranks)), device_id_type=MESH
        )
        return carry

    def greet_far(k, carry):
        pl.semaphore_signal(
            barrier, inc=1, device_id=(across, near_peer(k)), device_id_type=MESH
        )
        return carry

    lax.fori_loop(1, ranks, greet_group, 0)
    lax.fori_loop(0, deep, greet_far, 0)
    for neighbour in (after, before, sibling):
        pl.semaphore_signal(barrier, inc=1, device_id=(neighbour, t), device_id_type=MESH)

    def number(half):
        return jnp.right_shift(place_ref[pl.ds(half, 1), :], 7).astype(F32)

    def rotation(block_number, start, rows):
        step = lax.broadcasted_iota(jnp.int32, (rows, HEAD), 0) + start
        angle = (block_number * BLOCK + step.astype(F32)) * freq_ref[0:1, :]
        lane = lax.broadcasted_iota(jnp.int32, (rows, HEAD), 1)
        return jnp.cos(angle), jnp.where(lane < HEAD // 2, -1.0, 1.0) * jnp.sin(angle)

    for fetch in fetches[:3]:
        fetch.wait()
    cos_k, sin_k = rotation(
        number(lax.div(t, half_groups)), lax.rem(t, half_groups) * group, group
    )
    for h in range(ranks // 2):
        cols = slice(h * HEAD, (h + 1) * HEAD)
        place = (h % (wide // 2), h // (wide // 2))
        value = kv_ref[0, :, cols].astype(F32)
        turned = value * cos_k + pltpu.roll(value, HEAD // 2, 1) * sin_k
        staged[place[0], place[1], 0] = turned.astype(BF16)
        staged[place[0], place[1], 1] = kv_ref[1, :, cols]
    numbers[z] = jnp.broadcast_to(number(0), (16, HEAD)).astype(BF16)

    pl.semaphore_wait(barrier, ranks - 1 + deep + 3)

    def row_copy(k):
        peer = row_peer(k)
        return pltpu.make_async_remote_copy(
            src_ref=staged.at[lax.div(lax.rem(peer, wide), 2)],
            dst_ref=crossed.at[x],
            send_sem=x_send.at[k],
            recv_sem=x_recv.at[x],
            device_id=(c, peer),
            device_id_type=MESH,
        )

    def row_wait(k):
        pltpu.make_async_remote_copy(
            src_ref=staged.at[0],
            dst_ref=crossed.at[lax.rem(x + k, wide)],
            send_sem=x_send.at[k],
            recv_sem=x_recv.at[lax.rem(x + k, wide)],
            device_id=(c, row_peer(k)),
            device_id_type=MESH,
        ).wait_recv()

    def column_copy(k, target, part):
        peer = near_peer(k)
        return pltpu.make_async_remote_copy(
            src_ref=crossed.at[:, lax.div(peer, wide)],
            dst_ref=landed.at[z, pl.ds(low_z * wide, wide)],
            send_sem=z_send.at[part, k],
            recv_sem=z_recv.at[z, low_z],
            device_id=(target, peer),
            device_id_type=MESH,
        )

    def column_wait(zz, k):
        source = lax.rem(low_z + k, deep)
        pltpu.make_async_remote_copy(
            src_ref=crossed.at[:, 0],
            dst_ref=landed.at[zz, pl.ds(source * wide, wide)],
            send_sem=z_send.at[0, 0],
            recv_sem=z_recv.at[zz, source],
            device_id=(across, t),
            device_id_type=MESH,
        ).wait_recv()

    def id_copy(zz):
        return pltpu.make_async_remote_copy(
            src_ref=numbers.at[zz],
            dst_ref=numbers.at[zz],
            send_sem=m_send.at[0],
            recv_sem=m_recv.at[0],
            device_id=(across, t),
            device_id_type=MESH,
        )

    for k in range(1, wide):
        row_copy(k).start()
    id_copy(z).start()
    crossed[x] = staged[lax.div(x, 2)]
    for k in range(1, wide):
        row_wait(k)
    for k in range(1, deep):
        column_copy(k, c, 0).start()
    for k in range(deep):
        column_copy(k, across, 1).start()
    landed[z, pl.ds(low_z * wide, wide)] = crossed[:, low_z]

    def slot(k, way, s):
        return at(lax.rem(z + s, 2), turn(y + ring - (1 - 2 * way) * k), core)

    def move(where, layer, send, recv, target):
        low, size = LAYERS[layer]
        view = slab.at[where, pl.ds(low, size)]
        return pltpu.make_async_remote_copy(
            src_ref=view, dst_ref=view, send_sem=send, recv_sem=recv,
            device_id=(target, t), device_id_type=MESH,
        )

    def entry(way, s, layer):
        return 4 * way + 2 * s + layer

    def ring_copy(k, way, s, layer):
        e = entry(way, s, layer)
        target = at(z, turn(y + ring + 1 - 2 * way), core)
        return move(
            slot(k, way, s), layer, r_send.at[k, e], r_recv.at[k + 1, e], target
        )

    def ring_wait(k, way, s, layer):
        e = entry(way, s, layer)
        move(
            slot(k, way, s), layer, r_send.at[k, e], r_recv.at[k, e], after
        ).wait_recv()

    def goes_on(k, way, s):
        return jnp.logical_or(k < half_ring - 1, jnp.logical_and(k == half_ring - 1, s == way))

    def arrive(k, s, layer):
        for way in range(2):

            @pl.when(goes_on(k - 1, way, s))
            def _():
                ring_wait(k, way, s, layer)

                @pl.when(goes_on(k, way, s))
                def _():
                    ring_copy(k, way, s, layer).start()

    def arrange(zz):
        where = at(zz, y, core)
        first = numbers[zz].astype(F32)[0:1, :]
        smaller = first < blocks / 2
        halves = []
        for plane_index in range(2):
            pair = []
            for i in range(2):
                pieces = [
                    landed[zz, i * half_groups + g, plane_index] for g in range(half_groups)
                ]
                pair.append(jnp.concatenate(pieces, axis=0).astype(F32))
            halves.append(jnp.where(smaller, pair[0], pair[1]))
            halves.append(jnp.where(smaller, pair[1], pair[0]))
        slab[where, 0:BLOCK] = halves[0].T.astype(BF16)
        slab[where, BLOCK:2 * BLOCK] = halves[2].astype(BF16)
        low = jnp.minimum(first, blocks - 1 - first)
        slab[where, NUMBER:NUMBER + 16] = jnp.broadcast_to(low, (16, HEAD)).astype(BF16)
        slab[where, BIG:BIG + BLOCK] = halves[1].T.astype(BF16)
        slab[where, BIG + BLOCK:SLOT] = halves[3].astype(BF16)

    def launch(s):
        for layer in range(2):
            for way in range(2):
                if half_ring > 1 or s == way:
                    ring_copy(0, way, s, layer).start()

    first_id = number(0)
    first_small = first_id < blocks / 2
    fetches[3].wait()
    turns = [rotation(number(i), 0, BLOCK) for i in range(2)]
    for h in range(heads):
        rows = slice(h * BLOCK, (h + 1) * BLOCK)
        turned = []
        for i in range(2):
            value = queries[i * BLOCK:(i + 1) * BLOCK, h * HEAD:(h + 1) * HEAD].astype(F32)
            turned.append(value * turns[i][0] + pltpu.roll(value, HEAD // 2, 1) * turns[i][1])
        qq[1, rows, 0:HEAD] = jnp.where(first_small, turned[0], turned[1]).astype(BF16)
        qq[1, rows, HEAD:2 * HEAD] = jnp.where(first_small, turned[1], turned[0]).astype(BF16)
    qq[1, total:total + 16, :] = jnp.broadcast_to(
        jnp.concatenate([first_id, first_id], axis=1), (16, 2 * HEAD)
    ).astype(BF16)
    swap = pltpu.make_async_remote_copy(
        src_ref=qq.at[1], dst_ref=qq.at[0], send_sem=g_send.at[0], recv_sem=g_recv.at[0],
        device_id=(sibling, t), device_id_type=MESH,
    )
    swap.start()

    for k in range(1, deep):
        column_wait(z, k)
    arrange(z)
    launch(0)

    for k in range(deep):
        column_wait(1 - z, k)
    id_copy(1 - z).wait_recv()
    arrange(1 - z)
    launch(1)

    for best in (max_small, max_big):
        best[0] = jnp.full((total, HEAD), NEGATIVE, F32)
    for sums in (out_small, out_big):
        sums[0] = jnp.zeros((total, 2 * HEAD), F32)
    ones = jnp.ones((BLOCK, HEAD), BF16)
    token = lax.broadcasted_iota(jnp.int32, (BLOCK, BLOCK), 0)
    key = lax.broadcasted_iota(jnp.int32, (BLOCK, BLOCK), 1)

    def diagonal(h, carry):
        rows = pl.ds(pl.multiple_of(h * BLOCK, BLOCK), BLOCK)
        for i, (best, sums) in enumerate(((max_small, out_small), (max_big, out_big))):
            s = dot_nn(qq[1, rows, i * HEAD:(i + 1) * HEAD], slab[c, i * BIG:i * BIG + BLOCK])
            s = jnp.where(key <= token, s, NEGATIVE)
            m = jnp.max(s, axis=1, keepdims=True)
            best[1, rows, :] = jnp.broadcast_to(m, (BLOCK, HEAD))
            values = jnp.concatenate(
                [slab[c, i * BIG + BLOCK:i * BIG + 2 * BLOCK], ones], axis=1
            )
            sums[1, rows, :] = dot_nn(jnp.exp2((s - m) * scale).astype(BF16), values)
        return carry

    lax.fori_loop(0, heads, diagonal, 0)
    for i in range(4):
        for bank in range(4):
            vals_one[bank, i * BLOCK:(i + 1) * BLOCK, HEAD:2 * HEAD] = ones

    def flag(condition):
        return jnp.where(condition, 1.0, 0.0)

    def prepare(places, owner, bank):
        asker = qq[owner, total:total + 16, 0:HEAD].astype(F32)[0:1, :]
        my_small = jnp.minimum(asker, blocks - 1 - asker)
        for i, where in enumerate(places):
            small = slab[where, NUMBER:NUMBER + 16].astype(F32)[0:1, :]
            low = flag(small < my_small)
            high = flag(small > my_small)
            bias[bank, 2 * i] = jnp.broadcast_to((high - 1.0) * POSITIVE, (8, HEAD))
            bias[bank, 2 * i + 1] = jnp.broadcast_to((low - 1.0) * POSITIVE, (8, HEAD))
            low = low.astype(BF16)
            high = high.astype(BF16)
            span = slice(i * BLOCK, (i + 1) * BLOCK)
            k_small = slab[where, 0:BLOCK]
            k_big = slab[where, BIG:BIG + BLOCK]
            v_small = slab[where, BLOCK:2 * BLOCK]
            v_big = slab[where, BIG + BLOCK:SLOT]
            keys_one[bank, :, span] = k_small
            keys_two[bank, 0:HEAD, span] = k_small * low
            keys_two[bank, HEAD:2 * HEAD, span] = k_big * high
            vals_one[bank, span, 0:HEAD] = v_small
            vals_two[bank, span, 0:HEAD] = v_big * high
            vals_two[bank, span, HEAD:2 * HEAD] = ones * high
            vals_small[bank, span, 0:HEAD] = v_small * low
            vals_small[bank, span, HEAD:2 * HEAD] = ones * low

    def advance(n, owner, s, bank, own_slice=False):
        starts = range(s * half_rows, (s + 1) * half_rows, block_rows)
        keys = slice(0, n * BLOCK)
        bias_big = [bias[bank, 2 * i][0:1, :] for i in range(n)]
        bias_small = [bias[bank, 2 * i + 1][0:1, :] for i in range(n)]
        scores = []
        for start in starts:
            q = qq[owner, start:start + block_rows, :]
            scores.append((
                dot_nn(q[:, HEAD:2 * HEAD], keys_one[bank, :, keys]), dot_nn(q, keys_two[bank, :, keys])
            ))
        for start, (one, two) in zip(starts, scores):
            rows = slice(start, start + block_rows)
            ones_of = [one[:, i * BLOCK:(i + 1) * BLOCK] for i in range(n)]
            twos_of = [two[:, i * BLOCK:(i + 1) * BLOCK] for i in range(n)]
            big = functools.reduce(
                jnp.maximum, ones_of + [x + w for x, w in zip(twos_of, bias_big)]
            )
            small = functools.reduce(
                jnp.maximum, [x + w for x, w in zip(twos_of, bias_small)]
            )
            old_big = max_big[owner, rows, :]
            old_small = max_small[owner, rows, :]
            new_big = jnp.maximum(old_big, jnp.max(big, axis=1, keepdims=True))
            new_small = jnp.maximum(old_small, jnp.max(small, axis=1, keepdims=True))
            max_big[owner, rows, :] = new_big
            max_small[owner, rows, :] = new_small
            alpha_big = jnp.exp2((old_big - new_big) * scale)
            alpha_small = jnp.exp2((old_small - new_small) * scale)
            weights = [jnp.exp2((x - new_big) * scale).astype(BF16) for x in ones_of]
            later = []
            for x, wb, ws in zip(twos_of, bias_big, bias_small):
                m = new_small
                if own_slice:
                    m = jnp.where(ws == 0.0, m, POSITIVE)
                m = jnp.where(wb == 0.0, new_big, m)
                later.append(jnp.exp2((x - m) * scale).astype(BF16))
            later = jnp.concatenate(later, axis=1)
            every = jnp.concatenate(weights + [later], axis=1)
            values = jnp.concatenate([vals_one[bank, keys, :], vals_two[bank, keys, :]], axis=0)
            wide_big = jnp.concatenate([alpha_big, alpha_big], axis=1)
            wide_small = jnp.concatenate([alpha_small, alpha_small], axis=1)
            out_big[owner, rows, :] = out_big[owner, rows, :] * wide_big + dot_nn(every, values)
            out_small[owner, rows, :] = (
                out_small[owner, rows, :] * wide_small + dot_nn(later, vals_small[bank, keys, :])
            )

    half_heads = heads // 2
    half_rows = total // 2

    lane = lax.broadcasted_iota(jnp.int32, (BLOCK, HEAD), 1)
    log2_e = math.log2(math.e)

    def log_sum(best, weight):
        return best * scale + jnp.log(weight) * log2_e

    def part_copy(i):
        if i >= 2:
            src, dst = sums_out.at[i - 2], sums_in.at[i - 2]
        else:
            src = part_out.at[pl.ds(i * half_rows, half_rows)]
            dst = part_in.at[pl.ds(i * half_rows, half_rows)]
        return pltpu.make_async_remote_copy(
            src_ref=src, dst_ref=dst, send_sem=p_send.at[i], recv_sem=p_recv.at[i],
            device_id=(sibling, t), device_id_type=MESH,
        )

    def give_back(s):
        packed = jnp.zeros((BLOCK, HEAD), F32)
        for h in range(s * half_heads, (s + 1) * half_heads):
            rows = slice(h * BLOCK, (h + 1) * BLOCK)
            for i, (best, sums) in enumerate(((max_small, out_small), (max_big, out_big))):
                weight = jnp.maximum(sums[0, rows, HEAD:2 * HEAD], 1.0)
                part_out[rows, i * HEAD:(i + 1) * HEAD] = (
                    sums[0, rows, 0:HEAD] / weight
                ).astype(BF16)
                first = h * 16 + i * 8
                inside = jnp.logical_and(lane >= first, lane < first + 8)
                packed = jnp.where(inside, log_sum(best[0, rows, :], weight), packed)
        sums_out[s] = packed
        part_copy(s).start()
        part_copy(2 + s).start()

    width = half_heads * HEAD

    def columns(rank, s):
        return pl.ds(pl.multiple_of((2 * rank + s) * width, width), width)

    def tokens(rank):
        return pl.ds(pl.multiple_of(rank * group, group), group)

    def out_move(src, dst, s, send, recv, target):
        return pltpu.make_async_remote_copy(
            src_ref=done.at[tokens(src), pl.ds(s * width, width)],
            dst_ref=out_ref.at[:, columns(dst, s)],
            send_sem=o_send.at[send, s],
            recv_sem=o_recv.at[recv, s],
            device_id=(c, target),
            device_id_type=MESH,
        )

    def out_keep(s):
        return pltpu.make_async_copy(
            done.at[tokens(t), pl.ds(s * width, width)], out_ref.at[:, columns(t, s)], k_sem.at[s]
        )

    def finish(s):
        for h in range(s * half_heads, (s + 1) * half_heads):
            rows = slice(h * BLOCK, (h + 1) * BLOCK)
            cols = slice(h * HEAD, (h + 1) * HEAD)
            merged = []
            for i, (best, sums) in enumerate(((max_small, out_small), (max_big, out_big))):
                weight = sums[1, rows, HEAD:2 * HEAD]
                mine = log_sum(best[1, rows, :], weight)
                first = h * 16 + i * 8
                theirs = jnp.broadcast_to(sums_in[s, :, first:first + 1], (BLOCK, HEAD))
                top = jnp.maximum(mine, theirs)
                mine = jnp.exp2(mine - top)
                theirs = jnp.exp2(theirs - top)
                other_part = part_in[rows, i * HEAD:(i + 1) * HEAD].astype(F32)
                value = sums[1, rows, 0:HEAD] * (mine / weight) + other_part * theirs
                merged.append(value / (mine + theirs))
            small, big = merged
            done[0:BLOCK, cols] = jnp.where(first_small, small, big).astype(BF16)
            done[BLOCK:SLICE, cols] = jnp.where(first_small, big, small).astype(BF16)

        def out_start(k, carry):
            pt = lax.rem(t + k, ranks)
            out_move(pt, t, s, pt, t, pt).start()
            return carry

        lax.fori_loop(1, ranks, out_start, 0)
        out_keep(s).start()

    def near_places(k):
        return [slot(k, way, s) for way in range(2) for s in range(2)]

    swap.wait_recv()

    def first_step(owner, carry):
        prepare([slot(0, 0, s) for s in range(2)], owner, 0)
        for s in range(2):
            advance(2, owner, s, 0, True)
        return carry

    lax.fori_loop(0, 2, first_step, 0)
    for s in range(2):
        for layer in range(2):
            arrive(1, s, layer)

    def step(i, carry):
        k = lax.div(i, 2) + 1
        owner = lax.rem(i, 2)
        prepare(near_places(k), owner, 0)
        for s in range(2):
            advance(4, owner, s, 0)
            arrive(k + 1, owner, s)
        return carry

    if half_ring > 2:
        lax.fori_loop(0, 2 * (half_ring - 2), step, 0)

    places = near_places(half_ring - 1)
    last = [slot(half_ring, 0, s) for s in range(2)]
    for owner in range(2):
        prepare(places, owner, owner)
        advance(4, owner, 0, owner)
        for layer in range(2):
            arrive(half_ring, owner, layer)
    prepare(last, 0, 2)
    advance(2, 0, 0, 2)
    give_back(0)
    prepare(last, 1, 3)
    advance(2, 1, 0, 3)
    advance(4, 0, 1, 0)
    part_copy(0).wait_recv()
    part_copy(2).wait_recv()
    finish(0)
    advance(2, 0, 1, 2)
    give_back(1)
    advance(4, 1, 1, 1)
    advance(2, 1, 1, 3)
    part_copy(1).wait_recv()
    part_copy(3).wait_recv()
    finish(1)

    def ring_sent(k, carry):
        for way in range(2):
            for s in range(2):
                for layer in range(2):

                    @pl.when(goes_on(k, way, s))
                    def _():
                        ring_copy(k, way, s, layer).wait_send()

        return carry

    def out_sent(k, carry):
        pt = lax.rem(t + k, ranks)
        for s in range(2):
            out_move(pt, t, s, pt, t, pt).wait_send()
        return carry

    def out_wait(k, carry):
        pt = lax.rem(t + k, ranks)
        for s in range(2):
            out_move(t, pt, s, t, pt, pt).wait_recv()
        return carry

    for k in range(1, wide):
        row_copy(k).wait_send()
    for k in range(1, deep):
        column_copy(k, c, 0).wait_send()
    for k in range(deep):
        column_copy(k, across, 1).wait_send()
    id_copy(z).wait_send()
    lax.fori_loop(0, half_ring, ring_sent, 0)
    swap.wait_send()
    for i in range(4):
        part_copy(i).wait_send()
    for s in range(2):
        out_keep(s).wait()
    lax.fori_loop(1, ranks, out_sent, 0)
    lax.fori_loop(1, ranks, out_wait, 0)


def local(contexts, ranks, queries, key_value_rows, positions):
    heads = queries.shape[1] // HEAD
    group = SLICE // ranks
    ring = contexts // 4
    wide = min(4, ranks)
    deep = ranks // wide
    rows = heads * BLOCK
    block_rows = min(256, rows // 4)
    dma = pltpu.SemaphoreType.DMA
    return pl.pallas_call(
        functools.partial(kernel, contexts, ranks, heads, block_rows),
        out_shape=jax.ShapeDtypeStruct((group, ranks * heads * HEAD), BF16),
        in_specs=[pl.BlockSpec(memory_space=pltpu.HBM)] * 4,
        out_specs=pl.BlockSpec(memory_space=pltpu.HBM),
        scratch_shapes=[
            pltpu.VMEM((SLICE, heads * HEAD), BF16),
            pltpu.VMEM((2, group, ranks // 2 * HEAD), BF16),
            pltpu.VMEM((2, BLOCK), jnp.int32),
            pltpu.VMEM((8, HEAD), F32),
            pltpu.VMEM((2, ranks, 2, group, HEAD), BF16),
            pltpu.VMEM((2, 16, HEAD), BF16),
            pltpu.VMEM((contexts, SLOT, HEAD), BF16),
            pltpu.VMEM((wide // 2, deep, 2, group, HEAD), BF16),
            pltpu.VMEM((wide, deep, 2, group, HEAD), BF16),
            pltpu.VMEM((2, rows + 16, 2 * HEAD), BF16),
            pltpu.VMEM((4, HEAD, 4 * BLOCK), BF16),
            pltpu.VMEM((4, 2 * HEAD, 4 * BLOCK), BF16),
            pltpu.VMEM((4, 4 * BLOCK, 2 * HEAD), BF16),
            pltpu.VMEM((4, 4 * BLOCK, 2 * HEAD), BF16),
            pltpu.VMEM((4, 4 * BLOCK, 2 * HEAD), BF16),
            pltpu.VMEM((4, 8, 8, HEAD), F32),
            pltpu.VMEM((2, rows, 2 * HEAD), F32),
            pltpu.VMEM((2, rows, 2 * HEAD), F32),
            pltpu.VMEM((2, rows, HEAD), F32),
            pltpu.VMEM((2, rows, HEAD), F32),
            pltpu.VMEM((rows, 2 * HEAD), BF16),
            pltpu.VMEM((rows, 2 * HEAD), BF16),
            pltpu.VMEM((2, BLOCK, HEAD), F32),
            pltpu.VMEM((2, BLOCK, HEAD), F32),
            pltpu.VMEM((SLICE, heads * HEAD), BF16),
            dma((4,)),
            dma((wide,)),
            dma((wide,)),
            dma((2, deep)),
            dma((2, deep)),
            dma((1,)),
            dma((1,)),
            dma((ring // 2 + 1, 8)),
            dma((ring // 2 + 1, 8)),
            dma((1,)),
            dma((1,)),
            dma((4,)),
            dma((4,)),
            dma((ranks, 2)),
            dma((ranks, 2)),
            dma((2,)),
        ],
        compiler_params=pltpu.CompilerParams(
            collective_id=0, has_side_effects=True, vmem_limit_bytes=60 * 1024 * 1024
        ),
        cost_estimate=pl.CostEstimate(
            flops=8 * rows * SLICE * contexts * HEAD // 2,
            bytes_accessed=4 * 1024 * 1024,
            transcendentals=rows * SLICE * contexts,
        ),
    )(queries, key_value_rows, positions.reshape(2, BLOCK), jnp.asarray(frequencies(HEAD)))


def solution(mesh):
    placed = (P("context", "tensor"), P(None, ("context", "tensor"), None), P("context"))
    return jax.shard_map(
        functools.partial(local, mesh.shape["context"], mesh.shape["tensor"]),
        mesh=mesh,
        in_specs=placed,
        out_specs=P(("context", "tensor"), None),
        check_vma=False,
    )
```

```python
import functools
import math

import jax
import jax.numpy as jnp
import numpy as np
from jax import lax
from jax.experimental import pallas as pl
from jax.experimental.pallas import tpu as pltpu
from jax.sharding import PartitionSpec as P

HEAD = 128
BLOCK = 128
SLICE = 2 * BLOCK
NEGATIVE = -1e30
POSITIVE = 1e30
MESH = pl.DeviceIdType.MESH
F32 = jnp.float32
BF16 = jnp.bfloat16


NUMBER = 2 * BLOCK
BIG = 2 * BLOCK + 16
SLOT = 4 * BLOCK + 16
LAYER = SLOT // 3


def frequencies(width):
    counter = np.arange(width // 2, dtype=np.float32)
    inverse = np.float32(500000.0) ** (np.float32(-2.0) * counter / np.float32(width))
    wavelength = np.float32(2.0 * math.pi) / inverse
    smooth = np.clip((np.float32(8192.0) / wavelength - 1) / 3, 0, 1)
    f = (1 - smooth) * inverse / 8 + smooth * inverse
    return np.broadcast_to(np.concatenate([f, f])[None, :], (8, width)).astype(np.float32)


def dot_nn(a, b):
    return jnp.dot(a, b, preferred_element_type=F32)


def kernel(
    contexts, ranks, heads, block_rows,
    q_hbm, kv_hbm, place_hbm, freq_hbm, out_ref,
    queries, kv_ref, place_ref, freq_ref, landed, numbers, slab, staged, crossed,
    qq, keys_one, keys_two, vals_one, vals_two, vals_small, bias,
    out_big, out_small, max_big, max_small, part_out, part_in, sums_out, sums_in, done,
    in_sem, x_send, x_recv, z_send, z_recv, m_send, m_recv, r_send, r_recv, w_send, w_recv, g_send, g_recv, p_send, p_recv, o_send, o_recv, k_sem,
):
    ring = contexts // 4
    group = SLICE // ranks
    half_groups = ranks // 2
    wide = min(4, ranks)
    deep = ranks // wide
    blocks = 2 * contexts
    scale = math.log2(math.e) / math.sqrt(HEAD)
    total = heads * BLOCK

    c = lax.axis_index("context")
    t = lax.axis_index("tensor")
    core = lax.rem(c, 2)
    y = lax.rem(lax.div(c, 2), ring)
    z = lax.div(c, 2 * ring)
    half_ring = ring // 2

    def at(zz, yy, cc):
        return (zz * ring + yy) * 2 + cc

    def turn(v):
        return lax.rem(v + 2 * ring, ring)

    after = at(z, turn(y + 1), core)
    before = at(z, turn(y + ring - 1), core)
    sibling = at(z, y, 1 - core)
    across = at(1 - z, y, core)
    x = lax.rem(t, wide)
    low_z = lax.div(t, wide)
    odd = lax.rem(x, 2)
    twin = t + 1 - 2 * odd

    def row_peer(k):
        return low_z * wide + lax.rem(x + k, wide)

    def near_peer(k):
        return lax.rem(low_z + k, deep) * wide + x

    fetches = [
        pltpu.make_async_copy(src, dst, in_sem.at[i])
        for i, (src, dst) in enumerate((
            (place_hbm, place_ref), (freq_hbm, freq_ref), (kv_hbm, kv_ref), (q_hbm, queries)
        ))
    ]
    for fetch in fetches:
        fetch.start()

    barrier = pltpu.get_barrier_semaphore()

    def greet_group(k, carry):
        pl.semaphore_signal(
            barrier, inc=1, device_id=(c, lax.rem(t + k, ranks)), device_id_type=MESH
        )
        return carry

    def greet_far(k, carry):
        pl.semaphore_signal(
            barrier, inc=1, device_id=(across, near_peer(k)), device_id_type=MESH
        )
        return carry

    lax.fori_loop(1, ranks, greet_group, 0)
    lax.fori_loop(0, deep, greet_far, 0)
    for neighbour in (after, before, sibling):
        pl.semaphore_signal(barrier, inc=1, device_id=(neighbour, t), device_id_type=MESH)

    def number(half):
        return jnp.right_shift(place_ref[pl.ds(half, 1), :], 7).astype(F32)

    def rotation(block_number, start, rows):
        step = lax.broadcasted_iota(jnp.int32, (rows, HEAD), 0) + start
        angle = (block_number * BLOCK + step.astype(F32)) * freq_ref[0:1, :]
        lane = lax.broadcasted_iota(jnp.int32, (rows, HEAD), 1)
        return jnp.cos(angle), jnp.where(lane < HEAD // 2, -1.0, 1.0) * jnp.sin(angle)

    for fetch in fetches[:3]:
        fetch.wait()
    cos_k, sin_k = rotation(
        number(lax.div(t, half_groups)), lax.rem(t, half_groups) * group, group
    )
    for h in range(ranks // 2):
        cols = slice(h * HEAD, (h + 1) * HEAD)
        place = (h % (wide // 2), h // (wide // 2))
        value = kv_ref[0, :, cols].astype(F32)
        turned = value * cos_k + pltpu.roll(value, HEAD // 2, 1) * sin_k
        staged[place[0], place[1], 0] = turned.astype(BF16)
        staged[place[0], place[1], 1] = kv_ref[1, :, cols]
    numbers[z] = jnp.broadcast_to(number(0), (16, HEAD)).astype(BF16)

    pl.semaphore_wait(barrier, ranks - 1 + deep + 3)

    def row_copy(k):
        peer = row_peer(k)
        return pltpu.make_async_remote_copy(
            src_ref=staged.at[lax.div(lax.rem(peer, wide), 2)],
            dst_ref=crossed.at[x],
            send_sem=x_send.at[k],
            recv_sem=x_recv.at[x],
            device_id=(c, peer),
            device_id_type=MESH,
        )

    def row_wait(k):
        pltpu.make_async_remote_copy(
            src_ref=staged.at[0],
            dst_ref=crossed.at[lax.rem(x + k, wide)],
            send_sem=x_send.at[k],
            recv_sem=x_recv.at[lax.rem(x + k, wide)],
            device_id=(c, row_peer(k)),
            device_id_type=MESH,
        ).wait_recv()

    def column_copy(k, target, part):
        peer = near_peer(k)
        return pltpu.make_async_remote_copy(
            src_ref=crossed.at[:, lax.div(peer, wide)],
            dst_ref=landed.at[z, pl.ds(low_z * wide, wide)],
            send_sem=z_send.at[part, k],
            recv_sem=z_recv.at[z, low_z],
            device_id=(target, peer),
            device_id_type=MESH,
        )

    def column_wait(zz, k):
        source = lax.rem(low_z + k, deep)
        pltpu.make_async_remote_copy(
            src_ref=crossed.at[:, 0],
            dst_ref=landed.at[zz, pl.ds(source * wide, wide)],
            send_sem=z_send.at[0, 0],
            recv_sem=z_recv.at[zz, source],
            device_id=(across, t),
            device_id_type=MESH,
        ).wait_recv()

    def id_copy(zz):
        return pltpu.make_async_remote_copy(
            src_ref=numbers.at[zz],
            dst_ref=numbers.at[zz],
            send_sem=m_send.at[0],
            recv_sem=m_recv.at[0],
            device_id=(across, t),
            device_id_type=MESH,
        )

    for k in range(1, wide):
        row_copy(k).start()
    id_copy(z).start()
    crossed[x] = staged[lax.div(x, 2)]
    for k in range(1, wide):
        row_wait(k)
    for k in range(1, deep):
        column_copy(k, c, 0).start()
    for k in range(deep):
        column_copy(k, across, 1).start()
    landed[z, pl.ds(low_z * wide, wide)] = crossed[:, low_z]

    def slot(k, way, s):
        return at(lax.rem(z + s, 2), turn(y + ring - (1 - 2 * way) * k), core)

    def view(k, way, s, layer):
        start = pl.multiple_of(layer * LAYER, 16)
        return slab.at[slot(k, way, s), pl.ds(start, LAYER)]

    own = 1 + odd

    def ring_move(k, way, s, part, arrived):
        here = view(k, way, s, part * own)
        e = 4 * way + 2 * s + part
        return pltpu.make_async_remote_copy(
            src_ref=here, dst_ref=here, send_sem=r_send.at[k, e], recv_sem=r_recv.at[arrived, e],
            device_id=(at(z, turn(y + ring + 1 - 2 * way), core), t), device_id_type=MESH,
        )

    def ring_copy(k, way, s, part):
        return ring_move(k, way, s, part, k + 1)

    def ring_wait(k, way, s, part):
        ring_move(k, way, s, part, k).wait_recv()

    def twin_move(k, way, s, layer):
        here = view(k, way, s, layer)
        e = 2 * way + s
        return pltpu.make_async_remote_copy(
            src_ref=here, dst_ref=here, send_sem=w_send.at[k, e], recv_sem=w_recv.at[k, e],
            device_id=(c, twin), device_id_type=MESH,
        )

    def goes_on(k, way, s):
        return jnp.logical_or(k < half_ring - 1, jnp.logical_and(k == half_ring - 1, s == way))

    def arrive(k, s, part):
        for way in range(2):

            @pl.when(goes_on(k - 1, way, s))
            def _():
                ring_wait(k, way, s, part)

                @pl.when(goes_on(k, way, s))
                def _():
                    ring_copy(k, way, s, part).start()

                if part == 1:
                    twin_move(k, way, s, own).start()

    def arrive_twin(k, s):
        for way in range(2):

            @pl.when(goes_on(k - 1, way, s))
            def _():
                twin_move(k, way, s, 3 - own).wait_recv()

    def arrange(zz):
        where = at(zz, y, core)
        first = numbers[zz].astype(F32)[0:1, :]
        smaller = first < blocks / 2
        halves = []
        for plane_index in range(2):
            pair = []
            for i in range(2):
                pieces = [
                    landed[zz, i * half_groups + g, plane_index] for g in range(half_groups)
                ]
                pair.append(jnp.concatenate(pieces, axis=0).astype(F32))
            halves.append(jnp.where(smaller, pair[0], pair[1]))
            halves.append(jnp.where(smaller, pair[1], pair[0]))
        slab[where, 0:BLOCK] = halves[0].T.astype(BF16)
        slab[where, BLOCK:2 * BLOCK] = halves[2].astype(BF16)
        low = jnp.minimum(first, blocks - 1 - first)
        slab[where, NUMBER:NUMBER + 16] = jnp.broadcast_to(low, (16, HEAD)).astype(BF16)
        slab[where, BIG:BIG + BLOCK] = halves[1].T.astype(BF16)
        slab[where, BIG + BLOCK:SLOT] = halves[3].astype(BF16)

    def launch(s):
        for part in range(2):
            for way in range(2):
                if half_ring > 1 or s == way:
                    ring_copy(0, way, s, part).start()

    first_id = number(0)
    first_small = first_id < blocks / 2
    fetches[3].wait()
    turns = [rotation(number(i), 0, BLOCK) for i in range(2)]
    for h in range(heads):
        rows = slice(h * BLOCK, (h + 1) * BLOCK)
        turned = []
        for i in range(2):
            value = queries[i * BLOCK:(i + 1) * BLOCK, h * HEAD:(h + 1) * HEAD].astype(F32)
            turned.append(value * turns[i][0] + pltpu.roll(value, HEAD // 2, 1) * turns[i][1])
        qq[1, rows, 0:HEAD] = jnp.where(first_small, turned[0], turned[1]).astype(BF16)
        qq[1, rows, HEAD:2 * HEAD] = jnp.where(first_small, turned[1], turned[0]).astype(BF16)
    qq[1, total:total + 16, :] = jnp.broadcast_to(
        jnp.concatenate([first_id, first_id], axis=1), (16, 2 * HEAD)
    ).astype(BF16)
    swap = pltpu.make_async_remote_copy(
        src_ref=qq.at[1], dst_ref=qq.at[0], send_sem=g_send.at[0], recv_sem=g_recv.at[0],
        device_id=(sibling, t), device_id_type=MESH,
    )
    swap.start()

    for k in range(1, deep):
        column_wait(z, k)
    arrange(z)
    launch(0)

    for k in range(deep):
        column_wait(1 - z, k)
    id_copy(1 - z).wait_recv()
    arrange(1 - z)
    launch(1)

    for best in (max_small, max_big):
        best[0] = jnp.full((total, HEAD), NEGATIVE, F32)
    for sums in (out_small, out_big):
        sums[0] = jnp.zeros((total, 2 * HEAD), F32)
    ones = jnp.ones((BLOCK, HEAD), BF16)
    token = lax.broadcasted_iota(jnp.int32, (BLOCK, BLOCK), 0)
    key = lax.broadcasted_iota(jnp.int32, (BLOCK, BLOCK), 1)

    def diagonal(h, carry):
        rows = pl.ds(pl.multiple_of(h * BLOCK, BLOCK), BLOCK)
        for i, (best, sums) in enumerate(((max_small, out_small), (max_big, out_big))):
            s = dot_nn(qq[1, rows, i * HEAD:(i + 1) * HEAD], slab[c, i * BIG:i * BIG + BLOCK])
            s = jnp.where(key <= token, s, NEGATIVE)
            m = jnp.max(s, axis=1, keepdims=True)
            best[1, rows, :] = jnp.broadcast_to(m, (BLOCK, HEAD))
            values = jnp.concatenate(
                [slab[c, i * BIG + BLOCK:i * BIG + 2 * BLOCK], ones], axis=1
            )
            sums[1, rows, :] = dot_nn(jnp.exp2((s - m) * scale).astype(BF16), values)
        return carry

    lax.fori_loop(0, heads, diagonal, 0)
    for i in range(4):
        for bank in range(4):
            vals_one[bank, i * BLOCK:(i + 1) * BLOCK, HEAD:2 * HEAD] = ones

    def flag(condition):
        return jnp.where(condition, 1.0, 0.0)

    def prepare(places, owner, bank):
        asker = qq[owner, total:total + 16, 0:HEAD].astype(F32)[0:1, :]
        my_small = jnp.minimum(asker, blocks - 1 - asker)
        for i, where in enumerate(places):
            small = slab[where, NUMBER:NUMBER + 16].astype(F32)[0:1, :]
            low = flag(small < my_small)
            high = flag(small > my_small)
            bias[bank, 2 * i] = jnp.broadcast_to((high - 1.0) * POSITIVE, (8, HEAD))
            bias[bank, 2 * i + 1] = jnp.broadcast_to((low - 1.0) * POSITIVE, (8, HEAD))
            low = low.astype(BF16)
            high = high.astype(BF16)
            span = slice(i * BLOCK, (i + 1) * BLOCK)
            k_small = slab[where, 0:BLOCK]
            k_big = slab[where, BIG:BIG + BLOCK]
            v_small = slab[where, BLOCK:2 * BLOCK]
            v_big = slab[where, BIG + BLOCK:SLOT]
            keys_one[bank, :, span] = k_small
            keys_two[bank, 0:HEAD, span] = k_small * low
            keys_two[bank, HEAD:2 * HEAD, span] = k_big * high
            vals_one[bank, span, 0:HEAD] = v_small
            vals_two[bank, span, 0:HEAD] = v_big * high
            vals_two[bank, span, HEAD:2 * HEAD] = ones * high
            vals_small[bank, span, 0:HEAD] = v_small * low
            vals_small[bank, span, HEAD:2 * HEAD] = ones * low

    def advance(n, owner, s, bank, own_slice=False):
        starts = range(s * half_rows, (s + 1) * half_rows, block_rows)
        keys = slice(0, n * BLOCK)
        bias_big = [bias[bank, 2 * i][0:1, :] for i in range(n)]
        bias_small = [bias[bank, 2 * i + 1][0:1, :] for i in range(n)]
        scores = []
        for start in starts:
            q = qq[owner, start:start + block_rows, :]
            scores.append((
                dot_nn(q[:, HEAD:2 * HEAD], keys_one[bank, :, keys]), dot_nn(q, keys_two[bank, :, keys])
            ))
        for start, (one, two) in zip(starts, scores):
            rows = slice(start, start + block_rows)
            ones_of = [one[:, i * BLOCK:(i + 1) * BLOCK] for i in range(n)]
            twos_of = [two[:, i * BLOCK:(i + 1) * BLOCK] for i in range(n)]
            big = functools.reduce(
                jnp.maximum, ones_of + [x + w for x, w in zip(twos_of, bias_big)]
            )
            small = functools.reduce(
                jnp.maximum, [x + w for x, w in zip(twos_of, bias_small)]
            )
            old_big = max_big[owner, rows, :]
            old_small = max_small[owner, rows, :]
            new_big = jnp.maximum(old_big, jnp.max(big, axis=1, keepdims=True))
            new_small = jnp.maximum(old_small, jnp.max(small, axis=1, keepdims=True))
            max_big[owner, rows, :] = new_big
            max_small[owner, rows, :] = new_small
            alpha_big = jnp.exp2((old_big - new_big) * scale)
            alpha_small = jnp.exp2((old_small - new_small) * scale)
            weights = [jnp.exp2((x - new_big) * scale).astype(BF16) for x in ones_of]
            later = []
            for x, wb, ws in zip(twos_of, bias_big, bias_small):
                m = new_small
                if own_slice:
                    m = jnp.where(ws == 0.0, m, POSITIVE)
                m = jnp.where(wb == 0.0, new_big, m)
                later.append(jnp.exp2((x - m) * scale).astype(BF16))
            later = jnp.concatenate(later, axis=1)
            every = jnp.concatenate(weights + [later], axis=1)
            values = jnp.concatenate([vals_one[bank, keys, :], vals_two[bank, keys, :]], axis=0)
            wide_big = jnp.concatenate([alpha_big, alpha_big], axis=1)
            wide_small = jnp.concatenate([alpha_small, alpha_small], axis=1)
            out_big[owner, rows, :] = out_big[owner, rows, :] * wide_big + dot_nn(every, values)
            out_small[owner, rows, :] = (
                out_small[owner, rows, :] * wide_small + dot_nn(later, vals_small[bank, keys, :])
            )

    half_heads = heads // 2
    half_rows = total // 2

    lane = lax.broadcasted_iota(jnp.int32, (BLOCK, HEAD), 1)
    log2_e = math.log2(math.e)

    def log_sum(best, weight):
        return best * scale + jnp.log(weight) * log2_e

    def part_copy(i):
        if i >= 2:
            src, dst = sums_out.at[i - 2], sums_in.at[i - 2]
        else:
            src = part_out.at[pl.ds(i * half_rows, half_rows)]
            dst = part_in.at[pl.ds(i * half_rows, half_rows)]
        return pltpu.make_async_remote_copy(
            src_ref=src, dst_ref=dst, send_sem=p_send.at[i], recv_sem=p_recv.at[i],
            device_id=(sibling, t), device_id_type=MESH,
        )

    def give_back(s):
        packed = jnp.zeros((BLOCK, HEAD), F32)
        for h in range(s * half_heads, (s + 1) * half_heads):
            rows = slice(h * BLOCK, (h + 1) * BLOCK)
            for i, (best, sums) in enumerate(((max_small, out_small), (max_big, out_big))):
                weight = jnp.maximum(sums[0, rows, HEAD:2 * HEAD], 1.0)
                part_out[rows, i * HEAD:(i + 1) * HEAD] = (
                    sums[0, rows, 0:HEAD] / weight
                ).astype(BF16)
                first = h * 16 + i * 8
                inside = jnp.logical_and(lane >= first, lane < first + 8)
                packed = jnp.where(inside, log_sum(best[0, rows, :], weight), packed)
        sums_out[s] = packed
        part_copy(s).start()
        part_copy(2 + s).start()

    width = half_heads * HEAD

    def columns(rank, s):
        return pl.ds(pl.multiple_of((2 * rank + s) * width, width), width)

    def tokens(rank):
        return pl.ds(pl.multiple_of(rank * group, group), group)

    def out_move(src, dst, s, send, recv, target):
        return pltpu.make_async_remote_copy(
            src_ref=done.at[tokens(src), pl.ds(s * width, width)],
            dst_ref=out_ref.at[:, columns(dst, s)],
            send_sem=o_send.at[send, s],
            recv_sem=o_recv.at[recv, s],
            device_id=(c, target),
            device_id_type=MESH,
        )

    def out_keep(s):
        return pltpu.make_async_copy(
            done.at[tokens(t), pl.ds(s * width, width)], out_ref.at[:, columns(t, s)], k_sem.at[s]
        )

    def finish(s):
        for h in range(s * half_heads, (s + 1) * half_heads):
            rows = slice(h * BLOCK, (h + 1) * BLOCK)
            cols = slice(h * HEAD, (h + 1) * HEAD)
            merged = []
            for i, (best, sums) in enumerate(((max_small, out_small), (max_big, out_big))):
                weight = sums[1, rows, HEAD:2 * HEAD]
                mine = log_sum(best[1, rows, :], weight)
                first = h * 16 + i * 8
                theirs = jnp.broadcast_to(sums_in[s, :, first:first + 1], (BLOCK, HEAD))
                top = jnp.maximum(mine, theirs)
                mine = jnp.exp2(mine - top)
                theirs = jnp.exp2(theirs - top)
                other_part = part_in[rows, i * HEAD:(i + 1) * HEAD].astype(F32)
                value = sums[1, rows, 0:HEAD] * (mine / weight) + other_part * theirs
                merged.append(value / (mine + theirs))
            small, big = merged
            done[0:BLOCK, cols] = jnp.where(first_small, small, big).astype(BF16)
            done[BLOCK:SLICE, cols] = jnp.where(first_small, big, small).astype(BF16)

        def out_start(k, carry):
            pt = lax.rem(t + k, ranks)
            out_move(pt, t, s, pt, t, pt).start()
            return carry

        lax.fori_loop(1, ranks, out_start, 0)
        out_keep(s).start()

    def places(k):
        if k == 0 or k == half_ring:
            return [slot(k, 0, s) for s in range(2)]
        return [slot(k, way, s) for way in range(2) for s in range(2)]

    def take(k, s):
        for part in range(2):
            arrive(k, s, part)

    def take_twin(k):
        for s in range(2):
            arrive_twin(k, s)

    def compute(k, s):
        here = places(k)

        def both(owner, carry):
            bank = 2 * (k % 2) + owner
            if s == 0:
                prepare(here, owner, bank)
            advance(len(here), owner, s, bank, k == 0)
            return carry

        lax.fori_loop(0, 2, both, 0)

    swap.wait_recv()
    compute(0, 0)
    take(1, 0)
    take(1, 1)
    compute(0, 1)
    for k in range(1, half_ring):
        take(k + 1, 0)
        if k > 1:
            compute(k - 1, 1)
        take(k + 1, 1)
        take_twin(k)
        compute(k, 0)

    near = 2 * ((half_ring - 1) % 2)
    final = 2 - near
    last = places(half_ring)
    advance(4, 0, 1, near)
    take_twin(half_ring)
    for owner in range(2):
        prepare(last, owner, final + owner)
    advance(2, 0, 0, final)
    give_back(0)
    advance(2, 1, 0, final + 1)
    advance(2, 0, 1, final)
    give_back(1)
    part_copy(0).wait_recv()
    part_copy(2).wait_recv()
    finish(0)
    advance(4, 1, 1, near + 1)
    advance(2, 1, 1, final + 1)
    part_copy(1).wait_recv()
    part_copy(3).wait_recv()
    finish(1)

    def ring_sent(k, carry):
        for way in range(2):
            for s in range(2):

                @pl.when(goes_on(k, way, s))
                def _():
                    for part in range(2):
                        ring_copy(k, way, s, part).wait_send()
                    twin_move(k + 1, way, s, own).wait_send()

        return carry

    def out_sent(k, carry):
        pt = lax.rem(t + k, ranks)
        for s in range(2):
            out_move(pt, t, s, pt, t, pt).wait_send()
        return carry

    def out_wait(k, carry):
        pt = lax.rem(t + k, ranks)
        for s in range(2):
            out_move(t, pt, s, t, pt, pt).wait_recv()
        return carry

    for k in range(1, wide):
        row_copy(k).wait_send()
    for k in range(1, deep):
        column_copy(k, c, 0).wait_send()
    for k in range(deep):
        column_copy(k, across, 1).wait_send()
    id_copy(z).wait_send()
    lax.fori_loop(0, half_ring, ring_sent, 0)
    swap.wait_send()
    for i in range(4):
        part_copy(i).wait_send()
    for s in range(2):
        out_keep(s).wait()
    lax.fori_loop(1, ranks, out_sent, 0)
    lax.fori_loop(1, ranks, out_wait, 0)


def local(contexts, ranks, queries, key_value_rows, positions):
    heads = queries.shape[1] // HEAD
    group = SLICE // ranks
    ring = contexts // 4
    wide = min(4, ranks)
    deep = ranks // wide
    rows = heads * BLOCK
    block_rows = min(256, rows // 4)
    dma = pltpu.SemaphoreType.DMA
    return pl.pallas_call(
        functools.partial(kernel, contexts, ranks, heads, block_rows),
        out_shape=jax.ShapeDtypeStruct((group, ranks * heads * HEAD), BF16),
        in_specs=[pl.BlockSpec(memory_space=pltpu.HBM)] * 4,
        out_specs=pl.BlockSpec(memory_space=pltpu.HBM),
        scratch_shapes=[
            pltpu.VMEM((SLICE, heads * HEAD), BF16),
            pltpu.VMEM((2, group, ranks // 2 * HEAD), BF16),
            pltpu.VMEM((2, BLOCK), jnp.int32),
            pltpu.VMEM((8, HEAD), F32),
            pltpu.VMEM((2, ranks, 2, group, HEAD), BF16),
            pltpu.VMEM((2, 16, HEAD), BF16),
            pltpu.VMEM((contexts, SLOT, HEAD), BF16),
            pltpu.VMEM((wide // 2, deep, 2, group, HEAD), BF16),
            pltpu.VMEM((wide, deep, 2, group, HEAD), BF16),
            pltpu.VMEM((2, rows + 16, 2 * HEAD), BF16),
            pltpu.VMEM((4, HEAD, 4 * BLOCK), BF16),
            pltpu.VMEM((4, 2 * HEAD, 4 * BLOCK), BF16),
            pltpu.VMEM((4, 4 * BLOCK, 2 * HEAD), BF16),
            pltpu.VMEM((4, 4 * BLOCK, 2 * HEAD), BF16),
            pltpu.VMEM((4, 4 * BLOCK, 2 * HEAD), BF16),
            pltpu.VMEM((4, 8, 8, HEAD), F32),
            pltpu.VMEM((2, rows, 2 * HEAD), F32),
            pltpu.VMEM((2, rows, 2 * HEAD), F32),
            pltpu.VMEM((2, rows, HEAD), F32),
            pltpu.VMEM((2, rows, HEAD), F32),
            pltpu.VMEM((rows, 2 * HEAD), BF16),
            pltpu.VMEM((rows, 2 * HEAD), BF16),
            pltpu.VMEM((2, BLOCK, HEAD), F32),
            pltpu.VMEM((2, BLOCK, HEAD), F32),
            pltpu.VMEM((SLICE, heads * HEAD), BF16),
            dma((4,)),
            dma((wide,)),
            dma((wide,)),
            dma((2, deep)),
            dma((2, deep)),
            dma((1,)),
            dma((1,)),
            dma((ring // 2 + 1, 8)),
            dma((ring // 2 + 1, 8)),
            dma((ring // 2 + 1, 4)),
            dma((ring // 2 + 1, 4)),
            dma((1,)),
            dma((1,)),
            dma((4,)),
            dma((4,)),
            dma((ranks, 2)),
            dma((ranks, 2)),
            dma((2,)),
        ],
        compiler_params=pltpu.CompilerParams(
            collective_id=0, has_side_effects=True, vmem_limit_bytes=60 * 1024 * 1024
        ),
        cost_estimate=pl.CostEstimate(
            flops=8 * rows * SLICE * contexts * HEAD // 2,
            bytes_accessed=4 * 1024 * 1024,
            transcendentals=rows * SLICE * contexts,
        ),
    )(queries, key_value_rows, positions.reshape(2, BLOCK), jnp.asarray(frequencies(HEAD)))


def solution(mesh):
    placed = (P("context", "tensor"), P(None, ("context", "tensor"), None), P("context"))
    return jax.shard_map(
        functools.partial(local, mesh.shape["context"], mesh.shape["tensor"]),
        mesh=mesh,
        in_specs=placed,
        out_specs=P(("context", "tensor"), None),
        check_vma=False,
    )
```

```python
import functools
import math

import jax
import jax.numpy as jnp
import numpy as np
from jax import lax
from jax.experimental import pallas as pl
from jax.experimental.pallas import tpu as pltpu
from jax.sharding import PartitionSpec as P

HEAD = 128
BLOCK = 128
SLICE = 2 * BLOCK
NEGATIVE = -1e30
POSITIVE = 1e30
MESH = pl.DeviceIdType.MESH
F32 = jnp.float32
BF16 = jnp.bfloat16


LAYERS = ((0, 2 * BLOCK + 16), (2 * BLOCK + 16, 2 * BLOCK))
NUMBER = 2 * BLOCK
BIG = 2 * BLOCK + 16
SLOT = 4 * BLOCK + 16


def frequencies(width):
    counter = np.arange(width // 2, dtype=np.float32)
    inverse = np.float32(500000.0) ** (np.float32(-2.0) * counter / np.float32(width))
    wavelength = np.float32(2.0 * math.pi) / inverse
    smooth = np.clip((np.float32(8192.0) / wavelength - 1) / 3, 0, 1)
    f = (1 - smooth) * inverse / 8 + smooth * inverse
    return np.broadcast_to(np.concatenate([f, f])[None, :], (8, width)).astype(np.float32)


def dot_nn(a, b):
    return jnp.dot(a, b, preferred_element_type=F32)


def kernel(
    contexts, ranks, heads, block_rows,
    q_hbm, kv_hbm, place_hbm, freq_hbm, out_ref,
    queries, kv_ref, place_ref, freq_ref, landed, numbers, slab, staged, crossed,
    qq, keys_one, keys_two, vals_one, vals_two, vals_small, bias,
    out_big, out_small, max_big, max_small, part_out, part_in, sums_out, sums_in, done,
    in_sem, x_send, x_recv, z_send, z_recv, m_send, m_recv, r_send, r_recv, g_send, g_recv, p_send, p_recv, o_send, o_recv, k_sem,
):
    ring = contexts // 4
    group = SLICE // ranks
    half_groups = ranks // 2
    wide = min(4, ranks)
    deep = ranks // wide
    blocks = 2 * contexts
    scale = math.log2(math.e) / math.sqrt(HEAD)
    total = heads * BLOCK

    c = lax.axis_index("context")
    t = lax.axis_index("tensor")
    core = lax.rem(c, 2)
    y = lax.rem(lax.div(c, 2), ring)
    z = lax.div(c, 2 * ring)
    half_ring = ring // 2

    def at(zz, yy, cc):
        return (zz * ring + yy) * 2 + cc

    def turn(v):
        return lax.rem(v + 2 * ring, ring)

    after = at(z, turn(y + 1), core)
    before = at(z, turn(y + ring - 1), core)
    sibling = at(z, y, 1 - core)
    across = at(1 - z, y, core)
    x = lax.rem(t, wide)
    low_z = lax.div(t, wide)

    def row_peer(k):
        return low_z * wide + lax.rem(x + k, wide)

    def near_peer(k):
        return lax.rem(low_z + k, deep) * wide + x

    fetches = [
        pltpu.make_async_copy(src, dst, in_sem.at[i])
        for i, (src, dst) in enumerate((
            (place_hbm, place_ref), (freq_hbm, freq_ref), (kv_hbm, kv_ref), (q_hbm, queries)
        ))
    ]
    for fetch in fetches:
        fetch.start()

    barrier = pltpu.get_barrier_semaphore()

    def greet_group(k, carry):
        pl.semaphore_signal(
            barrier, inc=1, device_id=(c, lax.rem(t + k, ranks)), device_id_type=MESH
        )
        return carry

    def greet_far(k, carry):
        pl.semaphore_signal(
            barrier, inc=1, device_id=(across, near_peer(k)), device_id_type=MESH
        )
        return carry

    lax.fori_loop(1, ranks, greet_group, 0)
    lax.fori_loop(0, deep, greet_far, 0)
    for neighbour in (after, before, sibling):
        pl.semaphore_signal(barrier, inc=1, device_id=(neighbour, t), device_id_type=MESH)

    def number(half):
        return jnp.right_shift(place_ref[pl.ds(half, 1), :], 7).astype(F32)

    def rotation(block_number, start, rows):
        step = lax.broadcasted_iota(jnp.int32, (rows, HEAD), 0) + start
        angle = (block_number * BLOCK + step.astype(F32)) * freq_ref[0:1, :]
        lane = lax.broadcasted_iota(jnp.int32, (rows, HEAD), 1)
        return jnp.cos(angle), jnp.where(lane < HEAD // 2, -1.0, 1.0) * jnp.sin(angle)

    for fetch in fetches[:3]:
        fetch.wait()
    cos_k, sin_k = rotation(
        number(lax.div(t, half_groups)), lax.rem(t, half_groups) * group, group
    )
    for h in range(ranks // 2):
        cols = slice(h * HEAD, (h + 1) * HEAD)
        place = (h % (wide // 2), h // (wide // 2))
        value = kv_ref[0, :, cols].astype(F32)
        turned = value * cos_k + pltpu.roll(value, HEAD // 2, 1) * sin_k
        staged[place[0], place[1], 0] = turned.astype(BF16)
        staged[place[0], place[1], 1] = kv_ref[1, :, cols]
    numbers[z] = jnp.broadcast_to(number(0), (16, HEAD)).astype(BF16)

    pl.semaphore_wait(barrier, ranks - 1 + deep + 3)

    def row_copy(k):
        peer = row_peer(k)
        return pltpu.make_async_remote_copy(
            src_ref=staged.at[lax.div(lax.rem(peer, wide), 2)],
            dst_ref=crossed.at[x],
            send_sem=x_send.at[k],
            recv_sem=x_recv.at[x],
            device_id=(c, peer),
            device_id_type=MESH,
        )

    def row_wait(k):
        pltpu.make_async_remote_copy(
            src_ref=staged.at[0],
            dst_ref=crossed.at[lax.rem(x + k, wide)],
            send_sem=x_send.at[k],
            recv_sem=x_recv.at[lax.rem(x + k, wide)],
            device_id=(c, row_peer(k)),
            device_id_type=MESH,
        ).wait_recv()

    def column_copy(k, target, part):
        peer = near_peer(k)
        return pltpu.make_async_remote_copy(
            src_ref=crossed.at[:, lax.div(peer, wide)],
            dst_ref=landed.at[z, pl.ds(low_z * wide, wide)],
            send_sem=z_send.at[part, k],
            recv_sem=z_recv.at[z, low_z],
            device_id=(target, peer),
            device_id_type=MESH,
        )

    def column_wait(zz, k):
        source = lax.rem(low_z + k, deep)
        pltpu.make_async_remote_copy(
            src_ref=crossed.at[:, 0],
            dst_ref=landed.at[zz, pl.ds(source * wide, wide)],
            send_sem=z_send.at[0, 0],
            recv_sem=z_recv.at[zz, source],
            device_id=(across, t),
            device_id_type=MESH,
        ).wait_recv()

    def id_copy(zz):
        return pltpu.make_async_remote_copy(
            src_ref=numbers.at[zz],
            dst_ref=numbers.at[zz],
            send_sem=m_send.at[0],
            recv_sem=m_recv.at[0],
            device_id=(across, t),
            device_id_type=MESH,
        )

    for k in range(1, wide):
        row_copy(k).start()
    id_copy(z).start()
    crossed[x] = staged[lax.div(x, 2)]
    for k in range(1, wide):
        row_wait(k)
    for k in range(1, deep):
        column_copy(k, c, 0).start()
    for k in range(deep):
        column_copy(k, across, 1).start()
    landed[z, pl.ds(low_z * wide, wide)] = crossed[:, low_z]

    def slot(k, way, s):
        return at(lax.rem(z + s, 2), turn(y + ring - (1 - 2 * way) * k), core)

    def move(where, layer, send, recv, target):
        low, size = LAYERS[layer]
        view = slab.at[where, pl.ds(low, size)]
        return pltpu.make_async_remote_copy(
            src_ref=view, dst_ref=view, send_sem=send, recv_sem=recv,
            device_id=(target, t), device_id_type=MESH,
        )

    def entry(way, s, layer):
        return 4 * way + 2 * s + layer

    def ring_copy(k, way, s, layer):
        e = entry(way, s, layer)
        target = at(z, turn(y + ring + 1 - 2 * way), core)
        return move(
            slot(k, way, s), layer, r_send.at[k, e], r_recv.at[k + 1, e], target
        )

    def ring_wait(k, way, s, layer):
        e = entry(way, s, layer)
        move(
            slot(k, way, s), layer, r_send.at[k, e], r_recv.at[k, e], after
        ).wait_recv()

    def goes_on(k, way, s):
        return jnp.logical_or(k < half_ring - 1, jnp.logical_and(k == half_ring - 1, s == way))

    def arrive(k, s, layer):
        for way in range(2):

            @pl.when(goes_on(k - 1, way, s))
            def _():
                ring_wait(k, way, s, layer)

                @pl.when(goes_on(k, way, s))
                def _():
                    ring_copy(k, way, s, layer).start()

    def arrange(zz):
        where = at(zz, y, core)
        first = numbers[zz].astype(F32)[0:1, :]
        smaller = first < blocks / 2
        halves = []
        for plane_index in range(2):
            pair = []
            for i in range(2):
                pieces = [
                    landed[zz, i * half_groups + g, plane_index] for g in range(half_groups)
                ]
                pair.append(jnp.concatenate(pieces, axis=0).astype(F32))
            halves.append(jnp.where(smaller, pair[0], pair[1]))
            halves.append(jnp.where(smaller, pair[1], pair[0]))
        slab[where, 0:BLOCK] = halves[0].T.astype(BF16)
        slab[where, BLOCK:2 * BLOCK] = halves[2].astype(BF16)
        low = jnp.minimum(first, blocks - 1 - first)
        slab[where, NUMBER:NUMBER + 16] = jnp.broadcast_to(low, (16, HEAD)).astype(BF16)
        slab[where, BIG:BIG + BLOCK] = halves[1].T.astype(BF16)
        slab[where, BIG + BLOCK:SLOT] = halves[3].astype(BF16)

    def launch(s):
        for layer in range(2):
            for way in range(2):
                if half_ring > 1 or s == way:
                    ring_copy(0, way, s, layer).start()

    first_id = number(0)
    first_small = first_id < blocks / 2
    fetches[3].wait()
    turns = [rotation(number(i), 0, BLOCK) for i in range(2)]
    for h in range(heads):
        rows = slice(h * BLOCK, (h + 1) * BLOCK)
        turned = []
        for i in range(2):
            value = queries[i * BLOCK:(i + 1) * BLOCK, h * HEAD:(h + 1) * HEAD].astype(F32)
            turned.append(value * turns[i][0] + pltpu.roll(value, HEAD // 2, 1) * turns[i][1])
        qq[1, rows, 0:HEAD] = jnp.where(first_small, turned[0], turned[1]).astype(BF16)
        qq[1, rows, HEAD:2 * HEAD] = jnp.where(first_small, turned[1], turned[0]).astype(BF16)
    qq[1, total:total + 16, :] = jnp.broadcast_to(
        jnp.concatenate([first_id, first_id], axis=1), (16, 2 * HEAD)
    ).astype(BF16)
    swap = pltpu.make_async_remote_copy(
        src_ref=qq.at[1], dst_ref=qq.at[0], send_sem=g_send.at[0], recv_sem=g_recv.at[0],
        device_id=(sibling, t), device_id_type=MESH,
    )
    swap.start()

    for k in range(1, deep):
        column_wait(z, k)
    arrange(z)
    launch(0)

    for k in range(deep):
        column_wait(1 - z, k)
    id_copy(1 - z).wait_recv()
    arrange(1 - z)
    launch(1)

    for best in (max_small, max_big):
        best[0] = jnp.full((total, HEAD), NEGATIVE, F32)
    for sums in (out_small, out_big):
        sums[0] = jnp.zeros((total, 2 * HEAD), F32)
    ones = jnp.ones((BLOCK, HEAD), BF16)
    token = lax.broadcasted_iota(jnp.int32, (BLOCK, BLOCK), 0)
    key = lax.broadcasted_iota(jnp.int32, (BLOCK, BLOCK), 1)

    def diagonal(h, carry):
        rows = pl.ds(pl.multiple_of(h * BLOCK, BLOCK), BLOCK)
        for i, (best, sums) in enumerate(((max_small, out_small), (max_big, out_big))):
            s = dot_nn(qq[1, rows, i * HEAD:(i + 1) * HEAD], slab[c, i * BIG:i * BIG + BLOCK])
            s = jnp.where(key <= token, s, NEGATIVE)
            m = jnp.max(s, axis=1, keepdims=True)
            best[1, rows, :] = jnp.broadcast_to(m, (BLOCK, HEAD))
            values = jnp.concatenate(
                [slab[c, i * BIG + BLOCK:i * BIG + 2 * BLOCK], ones], axis=1
            )
            sums[1, rows, :] = dot_nn(jnp.exp2((s - m) * scale).astype(BF16), values)
        return carry

    lax.fori_loop(0, heads, diagonal, 0)
    for i in range(4):
        for bank in range(4):
            vals_one[bank, i * BLOCK:(i + 1) * BLOCK, HEAD:2 * HEAD] = ones

    def flag(condition):
        return jnp.where(condition, 1.0, 0.0)

    def prepare(places, owner, bank):
        asker = qq[owner, total:total + 16, 0:HEAD].astype(F32)[0:1, :]
        my_small = jnp.minimum(asker, blocks - 1 - asker)
        for i, where in enumerate(places):
            small = slab[where, NUMBER:NUMBER + 16].astype(F32)[0:1, :]
            low = flag(small < my_small)
            high = flag(small > my_small)
            bias[bank, 2 * i] = jnp.broadcast_to((high - 1.0) * POSITIVE, (8, HEAD))
            bias[bank, 2 * i + 1] = jnp.broadcast_to((low - 1.0) * POSITIVE, (8, HEAD))
            low = low.astype(BF16)
            high = high.astype(BF16)
            span = slice(i * BLOCK, (i + 1) * BLOCK)
            k_small = slab[where, 0:BLOCK]
            k_big = slab[where, BIG:BIG + BLOCK]
            v_small = slab[where, BLOCK:2 * BLOCK]
            v_big = slab[where, BIG + BLOCK:SLOT]
            keys_one[bank, :, span] = k_small
            keys_two[bank, 0:HEAD, span] = k_small * low
            keys_two[bank, HEAD:2 * HEAD, span] = k_big * high
            vals_one[bank, span, 0:HEAD] = v_small
            vals_two[bank, span, 0:HEAD] = v_big * high
            vals_two[bank, span, HEAD:2 * HEAD] = ones * high
            vals_small[bank, span, 0:HEAD] = v_small * low
            vals_small[bank, span, HEAD:2 * HEAD] = ones * low

    def advance(n, owner, s, bank, own_slice=False):
        starts = range(s * half_rows, (s + 1) * half_rows, block_rows)
        keys = slice(0, n * BLOCK)
        bias_big = [bias[bank, 2 * i][0:1, :] for i in range(n)]
        bias_small = [bias[bank, 2 * i + 1][0:1, :] for i in range(n)]
        scores = []
        for start in starts:
            q = qq[owner, start:start + block_rows, :]
            scores.append((
                dot_nn(q[:, HEAD:2 * HEAD], keys_one[bank, :, keys]), dot_nn(q, keys_two[bank, :, keys])
            ))
        for start, (one, two) in zip(starts, scores):
            rows = slice(start, start + block_rows)
            ones_of = [one[:, i * BLOCK:(i + 1) * BLOCK] for i in range(n)]
            twos_of = [two[:, i * BLOCK:(i + 1) * BLOCK] for i in range(n)]
            big = functools.reduce(
                jnp.maximum, ones_of + [x + w for x, w in zip(twos_of, bias_big)]
            )
            small = functools.reduce(
                jnp.maximum, [x + w for x, w in zip(twos_of, bias_small)]
            )
            old_big = max_big[owner, rows, :]
            old_small = max_small[owner, rows, :]
            new_big = jnp.maximum(old_big, jnp.max(big, axis=1, keepdims=True))
            new_small = jnp.maximum(old_small, jnp.max(small, axis=1, keepdims=True))
            max_big[owner, rows, :] = new_big
            max_small[owner, rows, :] = new_small
            alpha_big = jnp.exp2((old_big - new_big) * scale)
            alpha_small = jnp.exp2((old_small - new_small) * scale)
            weights = [jnp.exp2((x - new_big) * scale).astype(BF16) for x in ones_of]
            later = []
            for x, wb, ws in zip(twos_of, bias_big, bias_small):
                m = new_small
                if own_slice:
                    m = jnp.where(ws == 0.0, m, POSITIVE)
                m = jnp.where(wb == 0.0, new_big, m)
                later.append(jnp.exp2((x - m) * scale).astype(BF16))
            later = jnp.concatenate(later, axis=1)
            every = jnp.concatenate(weights + [later], axis=1)
            values = jnp.concatenate([vals_one[bank, keys, :], vals_two[bank, keys, :]], axis=0)
            wide_big = jnp.concatenate([alpha_big, alpha_big], axis=1)
            wide_small = jnp.concatenate([alpha_small, alpha_small], axis=1)
            out_big[owner, rows, :] = out_big[owner, rows, :] * wide_big + dot_nn(every, values)
            out_small[owner, rows, :] = (
                out_small[owner, rows, :] * wide_small + dot_nn(later, vals_small[bank, keys, :])
            )

    half_heads = heads // 2
    half_rows = total // 2

    lane = lax.broadcasted_iota(jnp.int32, (BLOCK, HEAD), 1)
    log2_e = math.log2(math.e)

    def log_sum(best, weight):
        return best * scale + jnp.log(weight) * log2_e

    def part_copy(i):
        if i >= 2:
            src, dst = sums_out.at[i - 2], sums_in.at[i - 2]
        else:
            src = part_out.at[pl.ds(i * half_rows, half_rows)]
            dst = part_in.at[pl.ds(i * half_rows, half_rows)]
        return pltpu.make_async_remote_copy(
            src_ref=src, dst_ref=dst, send_sem=p_send.at[i], recv_sem=p_recv.at[i],
            device_id=(sibling, t), device_id_type=MESH,
        )

    def give_back(s):
        packed = jnp.zeros((BLOCK, HEAD), F32)
        for h in range(s * half_heads, (s + 1) * half_heads):
            rows = slice(h * BLOCK, (h + 1) * BLOCK)
            for i, (best, sums) in enumerate(((max_small, out_small), (max_big, out_big))):
                weight = jnp.maximum(sums[0, rows, HEAD:2 * HEAD], 1.0)
                part_out[rows, i * HEAD:(i + 1) * HEAD] = (
                    sums[0, rows, 0:HEAD] / weight
                ).astype(BF16)
                first = h * 16 + i * 8
                inside = jnp.logical_and(lane >= first, lane < first + 8)
                packed = jnp.where(inside, log_sum(best[0, rows, :], weight), packed)
        sums_out[s] = packed
        part_copy(s).start()
        part_copy(2 + s).start()

    width = half_heads * HEAD

    def columns(rank, s):
        return pl.ds(pl.multiple_of((2 * rank + s) * width, width), width)

    def tokens(rank):
        return pl.ds(pl.multiple_of(rank * group, group), group)

    def out_move(src, dst, s, send, recv, target):
        return pltpu.make_async_remote_copy(
            src_ref=done.at[tokens(src), pl.ds(s * width, width)],
            dst_ref=out_ref.at[:, columns(dst, s)],
            send_sem=o_send.at[send, s],
            recv_sem=o_recv.at[recv, s],
            device_id=(c, target),
            device_id_type=MESH,
        )

    def out_keep(s):
        return pltpu.make_async_copy(
            done.at[tokens(t), pl.ds(s * width, width)], out_ref.at[:, columns(t, s)], k_sem.at[s]
        )

    def finish(s):
        for h in range(s * half_heads, (s + 1) * half_heads):
            rows = slice(h * BLOCK, (h + 1) * BLOCK)
            cols = slice(h * HEAD, (h + 1) * HEAD)
            merged = []
            for i, (best, sums) in enumerate(((max_small, out_small), (max_big, out_big))):
                weight = sums[1, rows, HEAD:2 * HEAD]
                mine = log_sum(best[1, rows, :], weight)
                first = h * 16 + i * 8
                theirs = jnp.broadcast_to(sums_in[s, :, first:first + 1], (BLOCK, HEAD))
                top = jnp.maximum(mine, theirs)
                mine = jnp.exp2(mine - top)
                theirs = jnp.exp2(theirs - top)
                other_part = part_in[rows, i * HEAD:(i + 1) * HEAD].astype(F32)
                value = sums[1, rows, 0:HEAD] * (mine / weight) + other_part * theirs
                merged.append(value / (mine + theirs))
            small, big = merged
            done[0:BLOCK, cols] = jnp.where(first_small, small, big).astype(BF16)
            done[BLOCK:SLICE, cols] = jnp.where(first_small, big, small).astype(BF16)

        def out_start(k, carry):
            pt = lax.rem(t + k, ranks)
            out_move(pt, t, s, pt, t, pt).start()
            return carry

        lax.fori_loop(1, ranks, out_start, 0)
        out_keep(s).start()

    def near_places(k):
        return [slot(k, way, s) for way in range(2) for s in range(2)]

    swap.wait_recv()

    def first_step(owner, carry):
        prepare([slot(0, 0, s) for s in range(2)], owner, 0)
        for s in range(2):
            advance(2, owner, s, 0, True)
        return carry

    lax.fori_loop(0, 2, first_step, 0)
    for s in range(2):
        for layer in range(2):
            arrive(1, s, layer)

    def step(i, carry):
        k = lax.div(i, 2) + 1
        owner = lax.rem(i, 2)
        prepare(near_places(k), owner, 0)
        for s in range(2):
            advance(4, owner, s, 0)
            arrive(k + 1, owner, s)
        return carry

    if half_ring > 2:
        lax.fori_loop(0, 2 * (half_ring - 2), step, 0)

    places = near_places(half_ring - 1)
    last = [slot(half_ring, 0, s) for s in range(2)]
    for owner in range(2):
        prepare(places, owner, owner)
        advance(4, owner, 0, owner)
        for layer in range(2):
            arrive(half_ring, owner, layer)
    prepare(last, 0, 2)
    advance(2, 0, 0, 2)
    give_back(0)
    prepare(last, 1, 3)
    advance(2, 1, 0, 3)
    advance(4, 0, 1, 0)
    part_copy(0).wait_recv()
    part_copy(2).wait_recv()
    finish(0)
    advance(2, 0, 1, 2)
    give_back(1)
    advance(4, 1, 1, 1)
    advance(2, 1, 1, 3)
    part_copy(1).wait_recv()
    part_copy(3).wait_recv()
    finish(1)

    def ring_sent(k, carry):
        for way in range(2):
            for s in range(2):
                for layer in range(2):

                    @pl.when(goes_on(k, way, s))
                    def _():
                        ring_copy(k, way, s, layer).wait_send()

        return carry

    def out_sent(k, carry):
        pt = lax.rem(t + k, ranks)
        for s in range(2):
            out_move(pt, t, s, pt, t, pt).wait_send()
        return carry

    def out_wait(k, carry):
        pt = lax.rem(t + k, ranks)
        for s in range(2):
            out_move(t, pt, s, t, pt, pt).wait_recv()
        return carry

    for k in range(1, wide):
        row_copy(k).wait_send()
    for k in range(1, deep):
        column_copy(k, c, 0).wait_send()
    for k in range(deep):
        column_copy(k, across, 1).wait_send()
    id_copy(z).wait_send()
    lax.fori_loop(0, half_ring, ring_sent, 0)
    swap.wait_send()
    for i in range(4):
        part_copy(i).wait_send()
    for s in range(2):
        out_keep(s).wait()
    lax.fori_loop(1, ranks, out_sent, 0)
    lax.fori_loop(1, ranks, out_wait, 0)


def local(contexts, ranks, queries, key_value_rows, positions):
    heads = queries.shape[1] // HEAD
    group = SLICE // ranks
    ring = contexts // 4
    wide = min(4, ranks)
    deep = ranks // wide
    rows = heads * BLOCK
    block_rows = min(512, rows // 2)
    dma = pltpu.SemaphoreType.DMA
    return pl.pallas_call(
        functools.partial(kernel, contexts, ranks, heads, block_rows),
        out_shape=jax.ShapeDtypeStruct((group, ranks * heads * HEAD), BF16),
        in_specs=[pl.BlockSpec(memory_space=pltpu.HBM)] * 4,
        out_specs=pl.BlockSpec(memory_space=pltpu.HBM),
        scratch_shapes=[
            pltpu.VMEM((SLICE, heads * HEAD), BF16),
            pltpu.VMEM((2, group, ranks // 2 * HEAD), BF16),
            pltpu.VMEM((2, BLOCK), jnp.int32),
            pltpu.VMEM((8, HEAD), F32),
            pltpu.VMEM((2, ranks, 2, group, HEAD), BF16),
            pltpu.VMEM((2, 16, HEAD), BF16),
            pltpu.VMEM((contexts, SLOT, HEAD), BF16),
            pltpu.VMEM((wide // 2, deep, 2, group, HEAD), BF16),
            pltpu.VMEM((wide, deep, 2, group, HEAD), BF16),
            pltpu.VMEM((2, rows + 16, 2 * HEAD), BF16),
            pltpu.VMEM((4, HEAD, 4 * BLOCK), BF16),
            pltpu.VMEM((4, 2 * HEAD, 4 * BLOCK), BF16),
            pltpu.VMEM((4, 4 * BLOCK, 2 * HEAD), BF16),
            pltpu.VMEM((4, 4 * BLOCK, 2 * HEAD), BF16),
            pltpu.VMEM((4, 4 * BLOCK, 2 * HEAD), BF16),
            pltpu.VMEM((4, 8, 8, HEAD), F32),
            pltpu.VMEM((2, rows, 2 * HEAD), F32),
            pltpu.VMEM((2, rows, 2 * HEAD), F32),
            pltpu.VMEM((2, rows, HEAD), F32),
            pltpu.VMEM((2, rows, HEAD), F32),
            pltpu.VMEM((rows, 2 * HEAD), BF16),
            pltpu.VMEM((rows, 2 * HEAD), BF16),
            pltpu.VMEM((2, BLOCK, HEAD), F32),
            pltpu.VMEM((2, BLOCK, HEAD), F32),
            pltpu.VMEM((SLICE, heads * HEAD), BF16),
            dma((4,)),
            dma((wide,)),
            dma((wide,)),
            dma((2, deep)),
            dma((2, deep)),
            dma((1,)),
            dma((1,)),
            dma((ring // 2 + 1, 8)),
            dma((ring // 2 + 1, 8)),
            dma((1,)),
            dma((1,)),
            dma((4,)),
            dma((4,)),
            dma((ranks, 2)),
            dma((ranks, 2)),
            dma((2,)),
        ],
        compiler_params=pltpu.CompilerParams(
            collective_id=0, has_side_effects=True, vmem_limit_bytes=60 * 1024 * 1024
        ),
        cost_estimate=pl.CostEstimate(
            flops=8 * rows * SLICE * contexts * HEAD // 2,
            bytes_accessed=4 * 1024 * 1024,
            transcendentals=rows * SLICE * contexts,
        ),
    )(queries, key_value_rows, positions.reshape(2, BLOCK), jnp.asarray(frequencies(HEAD)))


def solution(mesh):
    placed = (P("context", "tensor"), P(None, ("context", "tensor"), None), P("context"))
    return jax.shard_map(
        functools.partial(local, mesh.shape["context"], mesh.shape["tensor"]),
        mesh=mesh,
        in_specs=placed,
        out_specs=P(("context", "tensor"), None),
        check_vma=False,
    )
```

```python
import functools
import math

import jax
import jax.numpy as jnp
import numpy as np
from jax import lax
from jax.experimental import pallas as pl
from jax.experimental.pallas import tpu as pltpu
from jax.sharding import PartitionSpec as P

HEAD = 128
BLOCK = 128
SLICE = 2 * BLOCK
NEGATIVE = -1e30
POSITIVE = 1e30
MESH = pl.DeviceIdType.MESH
F32 = jnp.float32
BF16 = jnp.bfloat16


LAYERS = ((0, 2 * BLOCK + 16), (2 * BLOCK + 16, 2 * BLOCK))
NUMBER = 2 * BLOCK
BIG = 2 * BLOCK + 16
SLOT = 4 * BLOCK + 16


def frequencies(width):
    counter = np.arange(width // 2, dtype=np.float32)
    inverse = np.float32(500000.0) ** (np.float32(-2.0) * counter / np.float32(width))
    wavelength = np.float32(2.0 * math.pi) / inverse
    smooth = np.clip((np.float32(8192.0) / wavelength - 1) / 3, 0, 1)
    f = (1 - smooth) * inverse / 8 + smooth * inverse
    return np.broadcast_to(np.concatenate([f, f])[None, :], (8, width)).astype(np.float32)


def dot_nn(a, b):
    return jnp.dot(a, b, preferred_element_type=F32)


def kernel(
    contexts, ranks, heads, block_rows,
    q_hbm, kv_hbm, place_hbm, freq_hbm, out_ref,
    queries, kv_ref, place_ref, freq_ref, landed, numbers, slab, staged, crossed,
    qq, keys_one, keys_two, vals_one, vals_two, vals_small, bias,
    out_big, out_small, max_big, max_small, part_out, part_in, sums_out, sums_in, done,
    in_sem, x_send, x_recv, z_send, z_recv, m_send, m_recv, r_send, r_recv, g_send, g_recv, p_send, p_recv, o_send, o_recv, k_sem,
):
    ring = contexts // 4
    group = SLICE // ranks
    half_groups = ranks // 2
    wide = min(4, ranks)
    deep = ranks // wide
    blocks = 2 * contexts
    scale = math.log2(math.e) / math.sqrt(HEAD)
    total = heads * BLOCK

    c = lax.axis_index("context")
    t = lax.axis_index("tensor")
    core = lax.rem(c, 2)
    y = lax.rem(lax.div(c, 2), ring)
    z = lax.div(c, 2 * ring)
    half_ring = ring // 2

    def at(zz, yy, cc):
        return (zz * ring + yy) * 2 + cc

    def turn(v):
        return lax.rem(v + 2 * ring, ring)

    after = at(z, turn(y + 1), core)
    before = at(z, turn(y + ring - 1), core)
    sibling = at(z, y, 1 - core)
    across = at(1 - z, y, core)
    x = lax.rem(t, wide)
    low_z = lax.div(t, wide)

    def row_peer(k):
        return low_z * wide + lax.rem(x + k, wide)

    def near_peer(k):
        return lax.rem(low_z + k, deep) * wide + x

    fetches = [
        pltpu.make_async_copy(src, dst, in_sem.at[i])
        for i, (src, dst) in enumerate((
            (place_hbm, place_ref), (freq_hbm, freq_ref), (kv_hbm, kv_ref), (q_hbm, queries)
        ))
    ]
    for fetch in fetches:
        fetch.start()

    barrier = pltpu.get_barrier_semaphore()

    def greet_group(k, carry):
        pl.semaphore_signal(
            barrier, inc=1, device_id=(c, lax.rem(t + k, ranks)), device_id_type=MESH
        )
        return carry

    def greet_far(k, carry):
        pl.semaphore_signal(
            barrier, inc=1, device_id=(across, near_peer(k)), device_id_type=MESH
        )
        return carry

    lax.fori_loop(1, ranks, greet_group, 0)
    lax.fori_loop(0, deep, greet_far, 0)
    for neighbour in (after, before, sibling):
        pl.semaphore_signal(barrier, inc=1, device_id=(neighbour, t), device_id_type=MESH)

    def number(half):
        return jnp.right_shift(place_ref[pl.ds(half, 1), :], 7).astype(F32)

    def rotation(block_number, start, rows):
        step = lax.broadcasted_iota(jnp.int32, (rows, HEAD), 0) + start
        angle = (block_number * BLOCK + step.astype(F32)) * freq_ref[0:1, :]
        lane = lax.broadcasted_iota(jnp.int32, (rows, HEAD), 1)
        return jnp.cos(angle), jnp.where(lane < HEAD // 2, -1.0, 1.0) * jnp.sin(angle)

    for fetch in fetches[:3]:
        fetch.wait()
    cos_k, sin_k = rotation(
        number(lax.div(t, half_groups)), lax.rem(t, half_groups) * group, group
    )
    for h in range(ranks // 2):
        cols = slice(h * HEAD, (h + 1) * HEAD)
        place = (h % (wide // 2), h // (wide // 2))
        value = kv_ref[0, :, cols].astype(F32)
        turned = value * cos_k + pltpu.roll(value, HEAD // 2, 1) * sin_k
        staged[place[0], place[1], 0] = turned.astype(BF16)
        staged[place[0], place[1], 1] = kv_ref[1, :, cols]
    numbers[z] = jnp.broadcast_to(number(0), (16, HEAD)).astype(BF16)

    pl.semaphore_wait(barrier, ranks - 1 + deep + 3)

    def row_copy(k):
        peer = row_peer(k)
        return pltpu.make_async_remote_copy(
            src_ref=staged.at[lax.div(lax.rem(peer, wide), 2)],
            dst_ref=crossed.at[x],
            send_sem=x_send.at[k],
            recv_sem=x_recv.at[x],
            device_id=(c, peer),
            device_id_type=MESH,
        )

    def row_wait(k):
        pltpu.make_async_remote_copy(
            src_ref=staged.at[0],
            dst_ref=crossed.at[lax.rem(x + k, wide)],
            send_sem=x_send.at[k],
            recv_sem=x_recv.at[lax.rem(x + k, wide)],
            device_id=(c, row_peer(k)),
            device_id_type=MESH,
        ).wait_recv()

    def column_copy(k, target, part):
        peer = near_peer(k)
        return pltpu.make_async_remote_copy(
            src_ref=crossed.at[:, lax.div(peer, wide)],
            dst_ref=landed.at[z, pl.ds(low_z * wide, wide)],
            send_sem=z_send.at[part, k],
            recv_sem=z_recv.at[z, low_z],
            device_id=(target, peer),
            device_id_type=MESH,
        )

    def column_wait(zz, k):
        source = lax.rem(low_z + k, deep)
        pltpu.make_async_remote_copy(
            src_ref=crossed.at[:, 0],
            dst_ref=landed.at[zz, pl.ds(source * wide, wide)],
            send_sem=z_send.at[0, 0],
            recv_sem=z_recv.at[zz, source],
            device_id=(across, t),
            device_id_type=MESH,
        ).wait_recv()

    def id_copy(zz):
        return pltpu.make_async_remote_copy(
            src_ref=numbers.at[zz],
            dst_ref=numbers.at[zz],
            send_sem=m_send.at[0],
            recv_sem=m_recv.at[0],
            device_id=(across, t),
            device_id_type=MESH,
        )

    for k in range(1, wide):
        row_copy(k).start()
    id_copy(z).start()
    crossed[x] = staged[lax.div(x, 2)]
    for k in range(1, wide):
        row_wait(k)
    for k in range(1, deep):
        column_copy(k, c, 0).start()
    for k in range(deep):
        column_copy(k, across, 1).start()
    landed[z, pl.ds(low_z * wide, wide)] = crossed[:, low_z]

    def slot(k, way, s):
        return at(lax.rem(z + s, 2), turn(y + ring - (1 - 2 * way) * k), core)

    def move(where, layer, send, recv, target):
        low, size = LAYERS[layer]
        view = slab.at[where, pl.ds(low, size)]
        return pltpu.make_async_remote_copy(
            src_ref=view, dst_ref=view, send_sem=send, recv_sem=recv,
            device_id=(target, t), device_id_type=MESH,
        )

    def entry(way, s, layer):
        return 4 * way + 2 * s + layer

    def ring_copy(k, way, s, layer):
        e = entry(way, s, layer)
        target = at(z, turn(y + ring + 1 - 2 * way), core)
        return move(
            slot(k, way, s), layer, r_send.at[k, e], r_recv.at[k + 1, e], target
        )

    def ring_wait(k, way, s, layer):
        e = entry(way, s, layer)
        move(
            slot(k, way, s), layer, r_send.at[k, e], r_recv.at[k, e], after
        ).wait_recv()

    def goes_on(k, way, s):
        return jnp.logical_or(k < half_ring - 1, jnp.logical_and(k == half_ring - 1, s == way))

    def arrive(k, s, layer):
        for way in range(2):

            @pl.when(goes_on(k - 1, way, s))
            def _():
                ring_wait(k, way, s, layer)

                @pl.when(goes_on(k, way, s))
                def _():
                    ring_copy(k, way, s, layer).start()

    def arrange(zz):
        where = at(zz, y, core)
        first = numbers[zz].astype(F32)[0:1, :]
        smaller = first < blocks / 2
        halves = []
        for plane_index in range(2):
            pair = []
            for i in range(2):
                pieces = [
                    landed[zz, i * half_groups + g, plane_index] for g in range(half_groups)
                ]
                pair.append(jnp.concatenate(pieces, axis=0).astype(F32))
            halves.append(jnp.where(smaller, pair[0], pair[1]))
            halves.append(jnp.where(smaller, pair[1], pair[0]))
        slab[where, 0:BLOCK] = halves[0].T.astype(BF16)
        slab[where, BLOCK:2 * BLOCK] = halves[2].astype(BF16)
        low = jnp.minimum(first, blocks - 1 - first)
        slab[where, NUMBER:NUMBER + 16] = jnp.broadcast_to(low, (16, HEAD)).astype(BF16)
        slab[where, BIG:BIG + BLOCK] = halves[1].T.astype(BF16)
        slab[where, BIG + BLOCK:SLOT] = halves[3].astype(BF16)

    def launch(s):
        for layer in range(2):
            for way in range(2):
                if half_ring > 1 or s == way:
                    ring_copy(0, way, s, layer).start()

    first_id = number(0)
    first_small = first_id < blocks / 2
    fetches[3].wait()
    turns = [rotation(number(i), 0, BLOCK) for i in range(2)]
    for h in range(heads):
        rows = slice(h * BLOCK, (h + 1) * BLOCK)
        turned = []
        for i in range(2):
            value = queries[i * BLOCK:(i + 1) * BLOCK, h * HEAD:(h + 1) * HEAD].astype(F32)
            turned.append(value * turns[i][0] + pltpu.roll(value, HEAD // 2, 1) * turns[i][1])
        qq[1, rows, 0:HEAD] = jnp.where(first_small, turned[0], turned[1]).astype(BF16)
        qq[1, rows, HEAD:2 * HEAD] = jnp.where(first_small, turned[1], turned[0]).astype(BF16)
    qq[1, total:total + 16, :] = jnp.broadcast_to(
        jnp.concatenate([first_id, first_id], axis=1), (16, 2 * HEAD)
    ).astype(BF16)
    swap = pltpu.make_async_remote_copy(
        src_ref=qq.at[1], dst_ref=qq.at[0], send_sem=g_send.at[0], recv_sem=g_recv.at[0],
        device_id=(sibling, t), device_id_type=MESH,
    )
    swap.start()

    for k in range(1, deep):
        column_wait(z, k)
    arrange(z)
    launch(0)

    for k in range(deep):
        column_wait(1 - z, k)
    id_copy(1 - z).wait_recv()
    arrange(1 - z)
    launch(1)

    for best in (max_small, max_big):
        best[0] = jnp.full((total, HEAD), NEGATIVE, F32)
    for sums in (out_small, out_big):
        sums[0] = jnp.zeros((total, 2 * HEAD), F32)
    ones = jnp.ones((BLOCK, HEAD), BF16)
    token = lax.broadcasted_iota(jnp.int32, (BLOCK, BLOCK), 0)
    key = lax.broadcasted_iota(jnp.int32, (BLOCK, BLOCK), 1)

    def diagonal(h, carry):
        rows = pl.ds(pl.multiple_of(h * BLOCK, BLOCK), BLOCK)
        for i, (best, sums) in enumerate(((max_small, out_small), (max_big, out_big))):
            s = dot_nn(qq[1, rows, i * HEAD:(i + 1) * HEAD], slab[c, i * BIG:i * BIG + BLOCK])
            s = jnp.where(key <= token, s, NEGATIVE)
            m = jnp.max(s, axis=1, keepdims=True)
            best[1, rows, :] = jnp.broadcast_to(m, (BLOCK, HEAD))
            values = jnp.concatenate(
                [slab[c, i * BIG + BLOCK:i * BIG + 2 * BLOCK], ones], axis=1
            )
            sums[1, rows, :] = dot_nn(jnp.exp2((s - m) * scale).astype(BF16), values)
        return carry

    lax.fori_loop(0, heads, diagonal, 0)
    for i in range(4):
        for bank in range(4):
            vals_one[bank, i * BLOCK:(i + 1) * BLOCK, HEAD:2 * HEAD] = ones

    def flag(condition):
        return jnp.where(condition, 1.0, 0.0)

    def prepare(places, owner, bank):
        asker = qq[owner, total:total + 16, 0:HEAD].astype(F32)[0:1, :]
        my_small = jnp.minimum(asker, blocks - 1 - asker)
        for i, where in enumerate(places):
            small = slab[where, NUMBER:NUMBER + 16].astype(F32)[0:1, :]
            low = flag(small < my_small)
            high = flag(small > my_small)
            bias[bank, 2 * i] = jnp.broadcast_to((high - 1.0) * POSITIVE, (8, HEAD))
            bias[bank, 2 * i + 1] = jnp.broadcast_to((low - 1.0) * POSITIVE, (8, HEAD))
            low = low.astype(BF16)
            high = high.astype(BF16)
            span = slice(i * BLOCK, (i + 1) * BLOCK)
            k_small = slab[where, 0:BLOCK]
            k_big = slab[where, BIG:BIG + BLOCK]
            v_small = slab[where, BLOCK:2 * BLOCK]
            v_big = slab[where, BIG + BLOCK:SLOT]
            keys_one[bank, :, span] = k_small
            keys_two[bank, 0:HEAD, span] = k_small * low
            keys_two[bank, HEAD:2 * HEAD, span] = k_big * high
            vals_one[bank, span, 0:HEAD] = v_small
            vals_two[bank, span, 0:HEAD] = v_big * high
            vals_two[bank, span, HEAD:2 * HEAD] = ones * high
            vals_small[bank, span, 0:HEAD] = v_small * low
            vals_small[bank, span, HEAD:2 * HEAD] = ones * low

    def advance(n, owner, s, bank, own_slice=False):
        starts = range(s * half_rows, (s + 1) * half_rows, block_rows)
        keys = slice(0, n * BLOCK)
        bias_big = [bias[bank, 2 * i][0:1, :] for i in range(n)]
        bias_small = [bias[bank, 2 * i + 1][0:1, :] for i in range(n)]
        scores = []
        for start in starts:
            q = qq[owner, start:start + block_rows, :]
            scores.append((
                dot_nn(q[:, HEAD:2 * HEAD], keys_one[bank, :, keys]), dot_nn(q, keys_two[bank, :, keys])
            ))
        for start, (one, two) in zip(starts, scores):
            rows = slice(start, start + block_rows)
            ones_of = [one[:, i * BLOCK:(i + 1) * BLOCK] for i in range(n)]
            twos_of = [two[:, i * BLOCK:(i + 1) * BLOCK] for i in range(n)]
            big = functools.reduce(
                jnp.maximum, ones_of + [x + w for x, w in zip(twos_of, bias_big)]
            )
            small = functools.reduce(
                jnp.maximum, [x + w for x, w in zip(twos_of, bias_small)]
            )
            old_big = max_big[owner, rows, :]
            old_small = max_small[owner, rows, :]
            new_big = jnp.maximum(old_big, jnp.max(big, axis=1, keepdims=True))
            new_small = jnp.maximum(old_small, jnp.max(small, axis=1, keepdims=True))
            max_big[owner, rows, :] = new_big
            max_small[owner, rows, :] = new_small
            alpha_big = jnp.exp2((old_big - new_big) * scale)
            alpha_small = jnp.exp2((old_small - new_small) * scale)
            weights = [jnp.exp2((x - new_big) * scale).astype(BF16) for x in ones_of]
            later = []
            for x, wb, ws in zip(twos_of, bias_big, bias_small):
                m = new_small
                if own_slice:
                    m = jnp.where(ws == 0.0, m, POSITIVE)
                m = jnp.where(wb == 0.0, new_big, m)
                later.append(jnp.exp2((x - m) * scale).astype(BF16))
            later = jnp.concatenate(later, axis=1)
            every = jnp.concatenate(weights + [later], axis=1)
            values = jnp.concatenate([vals_one[bank, keys, :], vals_two[bank, keys, :]], axis=0)
            wide_big = jnp.concatenate([alpha_big, alpha_big], axis=1)
            wide_small = jnp.concatenate([alpha_small, alpha_small], axis=1)
            out_big[owner, rows, :] = out_big[owner, rows, :] * wide_big + dot_nn(every, values)
            out_small[owner, rows, :] = (
                out_small[owner, rows, :] * wide_small + dot_nn(later, vals_small[bank, keys, :])
            )

    half_heads = heads // 2
    half_rows = total // 2

    lane = lax.broadcasted_iota(jnp.int32, (BLOCK, HEAD), 1)
    log2_e = math.log2(math.e)

    def log_sum(best, weight):
        return best * scale + jnp.log(weight) * log2_e

    def part_copy(i):
        if i >= 2:
            src, dst = sums_out.at[i - 2], sums_in.at[i - 2]
        else:
            src = part_out.at[pl.ds(i * half_rows, half_rows)]
            dst = part_in.at[pl.ds(i * half_rows, half_rows)]
        return pltpu.make_async_remote_copy(
            src_ref=src, dst_ref=dst, send_sem=p_send.at[i], recv_sem=p_recv.at[i],
            device_id=(sibling, t), device_id_type=MESH,
        )

    def give_back(s):
        packed = jnp.zeros((BLOCK, HEAD), F32)
        for h in range(s * half_heads, (s + 1) * half_heads):
            rows = slice(h * BLOCK, (h + 1) * BLOCK)
            for i, (best, sums) in enumerate(((max_small, out_small), (max_big, out_big))):
                weight = jnp.maximum(sums[0, rows, HEAD:2 * HEAD], 1.0)
                part_out[rows, i * HEAD:(i + 1) * HEAD] = (
                    sums[0, rows, 0:HEAD] / weight
                ).astype(BF16)
                first = h * 16 + i * 8
                inside = jnp.logical_and(lane >= first, lane < first + 8)
                packed = jnp.where(inside, log_sum(best[0, rows, :], weight), packed)
        sums_out[s] = packed
        part_copy(s).start()
        part_copy(2 + s).start()

    width = half_heads * HEAD

    def columns(rank, s):
        return pl.ds(pl.multiple_of((2 * rank + s) * width, width), width)

    def tokens(rank):
        return pl.ds(pl.multiple_of(rank * group, group), group)

    def out_move(src, dst, s, send, recv, target):
        return pltpu.make_async_remote_copy(
            src_ref=done.at[tokens(src), pl.ds(s * width, width)],
            dst_ref=out_ref.at[:, columns(dst, s)],
            send_sem=o_send.at[send, s],
            recv_sem=o_recv.at[recv, s],
            device_id=(c, target),
            device_id_type=MESH,
        )

    def out_keep(s):
        return pltpu.make_async_copy(
            done.at[tokens(t), pl.ds(s * width, width)], out_ref.at[:, columns(t, s)], k_sem.at[s]
        )

    def finish(s):
        for h in range(s * half_heads, (s + 1) * half_heads):
            rows = slice(h * BLOCK, (h + 1) * BLOCK)
            cols = slice(h * HEAD, (h + 1) * HEAD)
            merged = []
            for i, (best, sums) in enumerate(((max_small, out_small), (max_big, out_big))):
                weight = sums[1, rows, HEAD:2 * HEAD]
                mine = log_sum(best[1, rows, :], weight)
                first = h * 16 + i * 8
                theirs = jnp.broadcast_to(sums_in[s, :, first:first + 1], (BLOCK, HEAD))
                top = jnp.maximum(mine, theirs)
                mine = jnp.exp2(mine - top)
                theirs = jnp.exp2(theirs - top)
                other_part = part_in[rows, i * HEAD:(i + 1) * HEAD].astype(F32)
                value = sums[1, rows, 0:HEAD] * (mine / weight) + other_part * theirs
                merged.append(value / (mine + theirs))
            small, big = merged
            done[0:BLOCK, cols] = jnp.where(first_small, small, big).astype(BF16)
            done[BLOCK:SLICE, cols] = jnp.where(first_small, big, small).astype(BF16)

        def out_start(k, carry):
            pt = lax.rem(t + k, ranks)
            out_move(pt, t, s, pt, t, pt).start()
            return carry

        edges = (1, max(ranks // 4, 1), max(ranks // 2, 1), ranks)
        for low, high in ((edges[2], edges[3]), (edges[1], edges[2]), (edges[0], edges[1])):
            lax.fori_loop(low, high, out_start, 0)
        out_keep(s).start()

    def near_places(k):
        return [slot(k, way, s) for way in range(2) for s in range(2)]

    swap.wait_recv()

    def first_step(owner, carry):
        prepare([slot(0, 0, s) for s in range(2)], owner, 0)
        for s in range(2):
            advance(2, owner, s, 0, True)
        return carry

    lax.fori_loop(0, 2, first_step, 0)
    for s in range(2):
        for layer in range(2):
            arrive(1, s, layer)

    def step(i, carry):
        k = lax.div(i, 2) + 1
        owner = lax.rem(i, 2)
        prepare(near_places(k), owner, 0)
        for s in range(2):
            advance(4, owner, s, 0)
            arrive(k + 1, owner, s)
        return carry

    if half_ring > 2:
        lax.fori_loop(0, 2 * (half_ring - 2), step, 0)

    places = near_places(half_ring - 1)
    last = [slot(half_ring, 0, s) for s in range(2)]
    for owner in range(2):
        prepare(places, owner, owner)
        advance(4, owner, 0, owner)
        for layer in range(2):
            arrive(half_ring, owner, layer)
    prepare(last, 0, 2)
    advance(2, 0, 0, 2)
    give_back(0)
    prepare(last, 1, 3)
    advance(2, 1, 0, 3)
    advance(4, 0, 1, 0)
    part_copy(0).wait_recv()
    part_copy(2).wait_recv()
    finish(0)
    advance(2, 0, 1, 2)
    give_back(1)
    advance(4, 1, 1, 1)
    advance(2, 1, 1, 3)
    part_copy(1).wait_recv()
    part_copy(3).wait_recv()
    finish(1)

    def ring_sent(k, carry):
        for way in range(2):
            for s in range(2):
                for layer in range(2):

                    @pl.when(goes_on(k, way, s))
                    def _():
                        ring_copy(k, way, s, layer).wait_send()

        return carry

    def out_sent(k, carry):
        pt = lax.rem(t + k, ranks)
        for s in range(2):
            out_move(pt, t, s, pt, t, pt).wait_send()
        return carry

    def out_wait(k, carry):
        pt = lax.rem(t + k, ranks)
        for s in range(2):
            out_move(t, pt, s, t, pt, pt).wait_recv()
        return carry

    for k in range(1, wide):
        row_copy(k).wait_send()
    for k in range(1, deep):
        column_copy(k, c, 0).wait_send()
    for k in range(deep):
        column_copy(k, across, 1).wait_send()
    id_copy(z).wait_send()
    lax.fori_loop(0, half_ring, ring_sent, 0)
    swap.wait_send()
    for i in range(4):
        part_copy(i).wait_send()
    for s in range(2):
        out_keep(s).wait()
    lax.fori_loop(1, ranks, out_sent, 0)
    lax.fori_loop(1, ranks, out_wait, 0)


def local(contexts, ranks, queries, key_value_rows, positions):
    heads = queries.shape[1] // HEAD
    group = SLICE // ranks
    ring = contexts // 4
    wide = min(4, ranks)
    deep = ranks // wide
    rows = heads * BLOCK
    block_rows = min(256, rows // 4)
    dma = pltpu.SemaphoreType.DMA
    return pl.pallas_call(
        functools.partial(kernel, contexts, ranks, heads, block_rows),
        out_shape=jax.ShapeDtypeStruct((group, ranks * heads * HEAD), BF16),
        in_specs=[pl.BlockSpec(memory_space=pltpu.HBM)] * 4,
        out_specs=pl.BlockSpec(memory_space=pltpu.HBM),
        scratch_shapes=[
            pltpu.VMEM((SLICE, heads * HEAD), BF16),
            pltpu.VMEM((2, group, ranks // 2 * HEAD), BF16),
            pltpu.VMEM((2, BLOCK), jnp.int32),
            pltpu.VMEM((8, HEAD), F32),
            pltpu.VMEM((2, ranks, 2, group, HEAD), BF16),
            pltpu.VMEM((2, 16, HEAD), BF16),
            pltpu.VMEM((contexts, SLOT, HEAD), BF16),
            pltpu.VMEM((wide // 2, deep, 2, group, HEAD), BF16),
            pltpu.VMEM((wide, deep, 2, group, HEAD), BF16),
            pltpu.VMEM((2, rows + 16, 2 * HEAD), BF16),
            pltpu.VMEM((4, HEAD, 4 * BLOCK), BF16),
            pltpu.VMEM((4, 2 * HEAD, 4 * BLOCK), BF16),
            pltpu.VMEM((4, 4 * BLOCK, 2 * HEAD), BF16),
            pltpu.VMEM((4, 4 * BLOCK, 2 * HEAD), BF16),
            pltpu.VMEM((4, 4 * BLOCK, 2 * HEAD), BF16),
            pltpu.VMEM((4, 8, 8, HEAD), F32),
            pltpu.VMEM((2, rows, 2 * HEAD), F32),
            pltpu.VMEM((2, rows, 2 * HEAD), F32),
            pltpu.VMEM((2, rows, HEAD), F32),
            pltpu.VMEM((2, rows, HEAD), F32),
            pltpu.VMEM((rows, 2 * HEAD), BF16),
            pltpu.VMEM((rows, 2 * HEAD), BF16),
            pltpu.VMEM((2, BLOCK, HEAD), F32),
            pltpu.VMEM((2, BLOCK, HEAD), F32),
            pltpu.VMEM((SLICE, heads * HEAD), BF16),
            dma((4,)),
            dma((wide,)),
            dma((wide,)),
            dma((2, deep)),
            dma((2, deep)),
            dma((1,)),
            dma((1,)),
            dma((ring // 2 + 1, 8)),
            dma((ring // 2 + 1, 8)),
            dma((1,)),
            dma((1,)),
            dma((4,)),
            dma((4,)),
            dma((ranks, 2)),
            dma((ranks, 2)),
            dma((2,)),
        ],
        compiler_params=pltpu.CompilerParams(
            collective_id=0, has_side_effects=True, vmem_limit_bytes=60 * 1024 * 1024
        ),
        cost_estimate=pl.CostEstimate(
            flops=8 * rows * SLICE * contexts * HEAD // 2,
            bytes_accessed=4 * 1024 * 1024,
            transcendentals=rows * SLICE * contexts,
        ),
    )(queries, key_value_rows, positions.reshape(2, BLOCK), jnp.asarray(frequencies(HEAD)))


def solution(mesh):
    placed = (P("context", "tensor"), P(None, ("context", "tensor"), None), P("context"))
    return jax.shard_map(
        functools.partial(local, mesh.shape["context"], mesh.shape["tensor"]),
        mesh=mesh,
        in_specs=placed,
        out_specs=P(("context", "tensor"), None),
        check_vma=False,
    )
```
